512 devices in a mesh: expert: 64 (over z, y), dp: 8 (over x, core).
Axes of the slice: x: 4, y: 4, z: 16, core: 2. Of those that a mesh axis runs over, the one named last changes fastest.
Arguments:
- tokens: bfloat16 [2, 2048, 7168], P(None, 'expert'), may hold values from -6 to 6
- routes: int32 [2, 2048, 2], P(None, 'expert'), may hold values from 0 to 3, all different within a row
- mix_weights: float32 [2, 2048, 2], P(None, 'expert'), may hold values from 0.2 to 1
- up_partial: bfloat16 [8, 64, 448, 1024], P('dp', 'expert'), may hold values from -6 to 6
- down_partial: bfloat16 [8, 64, 64, 7168], P('dp', 'expert'), may hold values from -6 to 6
- up_master: float32 [64, 448, 1024], P('expert', None, 'dp'), may hold values from -0.0625 to 0.0625
- down_master: float32 [64, 64, 7168], P('expert', None, 'dp'), may hold values from -0.1875 to 0.1875
- up_first: float32 [64, 448, 1024], P('expert', None, 'dp'), may hold values from -0.0017089844 to 0.0017089844
- down_first: float32 [64, 64, 7168], P('expert', None, 'dp'), may hold values from -0.0017089844 to 0.0017089844
- up_second: float32 [64, 448, 1024], P('expert', None, 'dp'), may hold values from 1e-07 to 1e-06
- down_second: float32 [64, 64, 7168], P('expert', None, 'dp'), may hold values from 1e-07 to 1e-06
- counts: int32 [8, 4], P('dp'), may hold values from 32 to 1023
- owner_key: int32 [1], replicated, may hold values from 0 to 63
Outputs:
- up_update: float32 [64, 448, 1024], P('expert', None, 'dp')
- down_update: float32 [64, 64, 7168], P('expert', None, 'dp')
- decoded: bfloat16 [2, 2048, 7168], P(None, 'expert', 'dp')
The draws below stay inside these ranges and needn't reach their ends.
Inputs may be any that keep to these rules, and one draw needn't show every extreme that they name: `routes`: each row names 2 different experts.
All inputs are finite; a program needn't handle non-finite values.
Results may differ from the reference program's by a relative error of at most 0.014.
Values may be sent and summed in bfloat16 or wider, within the bound.
A program may use at most 64 MiB of HBM per device.

```python
import math
import jax
import jax.numpy as jnp
from jax import lax

D = 7168
FW = 1024
EXPERTS = 4
TOP = 2
STEPS = 2
DS = 448
US = 64
ROWS = 2048
N_EXPERT = 64
N_DP = 8


def place_ends(result, key, smallest, top_value):
    extent = result.shape
    spot = [jax.random.randint(jax.random.fold_in(key, axis), (), 0, extent[axis]) for axis in range(len(extent))]
    result = result.at[tuple(spot)].set(smallest)
    longest = extent.index(max(extent))
    spot[longest] = (spot[longest] + 1) % extent[longest]
    return result.at[tuple(spot)].set(top_value)


def block_scale(rng, extent, shards, least, largest):
    factor_of, own = 1.0, jax.random.fold_in(rng, 6)
    for position, parts in shards:
        heights = jnp.exp(jax.random.uniform(jax.random.fold_in(own, position), (parts,), jnp.float32, least / len(shards), largest / len(shards)))
        factor_of = factor_of * jnp.repeat(heights, extent[position] // parts).reshape([-1 if axis == position else 1 for axis in range(len(extent))])
    return factor_of


def distinct(own_key, rows, count, top, lift):
    ranking = jax.random.permutation(jax.random.fold_in(own_key, 1), count)
    pull = ranking
    for power in range(3):
        pull = pull * pull // count
    pull = pull * lift // count
    lots = jax.random.randint(jax.random.fold_in(own_key, 2), (rows, count), 0, 4096) + pull
    fixed_rows = jax.random.permutation(jax.random.fold_in(own_key, 3), rows)[jnp.arange(count) % rows]
    lots = jnp.where(jnp.arange(rows)[:, None] == fixed_rows[None, :], 1 << 14, lots)
    priority = lots * count + jnp.arange(count)
    return lax.top_k(priority.astype(jnp.int32), top)[1].astype(jnp.int32)


def gaussian(rng, shape, scale, reach, shards=(), held_as=jnp.bfloat16):
    level = block_scale(rng, shape, shards, -0.22, 0.18) if shards else 1.0
    drawn = jax.random.normal(rng, shape, jnp.float32) * scale * level
    return jnp.minimum(jnp.maximum(drawn, -reach), reach).astype(held_as)


def setup_inputs(seed: int = 0) -> dict:
    seeds = jax.random.split(jax.random.key(seed), 14)
    return {
        "tokens": gaussian(seeds[0], (STEPS, ROWS, D), 1.0, 6.0, ((1, 64),)),
        "routes": distinct(seeds[1], STEPS * ROWS, EXPERTS, TOP, 8192).reshape((STEPS, ROWS, TOP)),
        "mix_weights": jnp.clip(0.2 + 0.8 * jax.random.uniform(seeds[2], (STEPS, ROWS, TOP), jnp.float32) ** block_scale(seeds[2], (STEPS, ROWS, TOP), ((1, 64),), -0.2, 0.2), 0.2, 1.0),
        "up_partial": gaussian(seeds[3], (N_DP, N_EXPERT, DS, FW), 1.0, 6.0, ((0, 8), (1, 64))),
        "down_partial": gaussian(seeds[4], (N_DP, N_EXPERT, US, D), 1.0, 6.0, ((0, 8), (1, 64))),
        "up_master": gaussian(seeds[5], (N_EXPERT, DS, FW), D ** -0.5, 0.0625, ((0, 64), (2, 8)), jnp.float32),
        "down_master": gaussian(seeds[6], (N_EXPERT, US, D), FW ** -0.5, 0.1875, ((0, 64), (2, 8)), jnp.float32),
        "up_first": gaussian(seeds[7], (N_EXPERT, DS, FW), 0.0003, 0.0017089844, ((0, 64), (2, 8)), jnp.float32),
        "down_first": gaussian(seeds[8], (N_EXPERT, US, D), 0.0003, 0.0017089844, ((0, 64), (2, 8)), jnp.float32),
        "up_second": jnp.clip(jnp.exp(math.log(9.999999974752427e-07) - 2.3025851 * jax.random.uniform(seeds[9], (N_EXPERT, DS, FW), jnp.float32) ** block_scale(seeds[9], (N_EXPERT, DS, FW), ((0, 64), (2, 8)), -0.2, 0.2)), 1.0000000116860974e-07, 9.999999974752427e-07),
        "down_second": jnp.clip(jnp.exp(math.log(9.999999974752427e-07) - 2.3025851 * jax.random.uniform(seeds[10], (N_EXPERT, US, D), jnp.float32) ** block_scale(seeds[10], (N_EXPERT, US, D), ((0, 64), (2, 8)), -0.2, 0.2)), 1.0000000116860974e-07, 9.999999974752427e-07),
        "counts": place_ends(jax.random.randint(seeds[11], (N_DP, EXPERTS), 32, 1024), jax.random.fold_in(seeds[11], 1), 32, 1023).astype(jnp.int32),
        "owner_key": jax.random.randint(seeds[12], (1,), 0, N_EXPERT).astype(jnp.int32),
    }


beta_one = 0.9
beta_two = 0.95
first_fix = 1.0 - 0.9 ** 10
second_fix = 1.0 - 0.95 ** 10
epsilon = 1e-08
weight_decay = 0.1
learn_rate = 0.001

def adamw_step(gradient, weight, first, second):
    first_new = beta_one * first + (1.0 - beta_one) * gradient
    second_new = beta_two * second + (1.0 - beta_two) * gradient * gradient
    update = first_new / first_fix / (jnp.sqrt(second_new / second_fix) + epsilon) + weight_decay * weight
    return (update, weight - learn_rate * update)

def reference(tokens, routes, mix_weights, up_partial, down_partial, up_master, down_master, up_first, down_first, up_second, down_second, counts, owner_key):
    totals = lax.optimization_barrier(jnp.sum(counts, axis=0, dtype=jnp.int32))
    blocks = jnp.bitwise_xor(jnp.arange(N_EXPERT, dtype=jnp.int32), owner_key[0])
    owners = blocks // (N_EXPERT // EXPERTS)
    divisor = jnp.take(totals, owners).astype(jnp.float32)
    up_grad = lax.optimization_barrier(jnp.sum(up_partial.astype(jnp.float32), axis=0)) / divisor[:, None, None]
    down_grad = lax.optimization_barrier(jnp.sum(down_partial.astype(jnp.float32), axis=0)) / divisor[:, None, None]
    up_update, up_new = adamw_step(up_grad, up_master, up_first, up_second)
    down_update, down_new = adamw_step(down_grad, down_master, down_first, down_second)
    up_serve = jnp.take(up_new.astype(jnp.bfloat16), blocks, axis=0).reshape(EXPERTS, D, FW)
    down_serve = jnp.take(down_new.astype(jnp.bfloat16), blocks, axis=0).reshape(EXPERTS, FW, D)
    labels = jnp.arange(EXPERTS, dtype=jnp.int32)
    matches = routes[..., None] == labels
    gates = lax.optimization_barrier(jnp.sum(jnp.where(matches, mix_weights[..., None], 0.0), axis=2))
    flat_rows = tokens.reshape(STEPS * ROWS, D)

    def expert_out(pair):
        up_weight, down_weight = pair
        hidden = jax.nn.silu(jnp.dot(flat_rows, up_weight, preferred_element_type=jnp.float32)).astype(jnp.bfloat16)
        return jnp.dot(hidden, down_weight, preferred_element_type=jnp.float32).astype(jnp.bfloat16)
    expert_rows = lax.map(expert_out, (up_serve, down_serve))
    mixed = jnp.einsum('ne,end->nd', gates.reshape(STEPS * ROWS, EXPERTS), expert_rows.astype(jnp.float32))
    decoded = mixed.reshape(STEPS, ROWS, D).astype(jnp.bfloat16)
    return (up_update, down_update, decoded)
```

```python
import jax
import jax.numpy as jnp
from jax import lax
from jax.sharding import PartitionSpec as P

EXPERTS = 4


beta_one = 0.9
beta_two = 0.95
first_fix = 1.0 - 0.9**10
second_fix = 1.0 - 0.95**10
epsilon = 1e-08
weight_decay = 0.1
learn_rate = 0.001


def partner_2(x, axis, distance):
    return lax.ppermute(x, axis, [(i, i ^ 1 << distance) for i in range(lax.axis_size(axis))])


def adamw_step(gradient, weight, first, second):
    first_new = beta_one * first + (1.0 - beta_one) * gradient
    second_new = beta_two * second + (1.0 - beta_two) * gradient * gradient
    update = (
        first_new / first_fix / (jnp.sqrt(second_new / second_fix) + epsilon)
        + weight_decay * weight
    )
    return (update, weight - learn_rate * update)


def gather_group(piece, replicas):
    position = lax.axis_index("expert")
    holding = piece[None]
    for level in range(replicas.bit_length() - 1):
        partner = partner_2(holding, "expert", level)
        upper = jnp.bitwise_and(jnp.right_shift(position, level), 1)
        holding = jnp.where(
            upper == 1,
            jnp.concatenate([partner, holding], 0),
            jnp.concatenate([holding, partner], 0),
        )
    return holding


def per_device(
    tokens,
    routes,
    mix_weights,
    up_partial,
    down_partial,
    up_master,
    down_master,
    up_first,
    down_first,
    up_second,
    down_second,
    counts,
    owner_key,
):
    peer_count = lax.axis_size("expert")
    replicas = peer_count // EXPERTS
    position = lax.axis_index("expert")
    owner = owner_key[0]
    block = jnp.bitwise_xor(position, owner)
    totals = lax.psum(counts[0], "dp")
    labels = jnp.arange(EXPERTS, dtype=jnp.int32)
    row_count = jnp.sum(jnp.where(labels == block // replicas, totals, 0)).astype(jnp.float32)
    up_sum, down_sum = (
        lax.psum_scatter(up_partial[0, 0], "dp", scatter_dimension=1, tiled=True).astype(
            jnp.float32
        ),
        lax.psum_scatter(down_partial[0, 0], "dp", scatter_dimension=1, tiled=True).astype(
            jnp.float32
        ),
    )
    up_update, up_new = adamw_step(up_sum / row_count, up_master[0], up_first[0], up_second[0])
    down_update, down_new = adamw_step(
        down_sum / row_count, down_master[0], down_first[0], down_second[0]
    )
    piece = jnp.stack(
        [up_new.astype(jnp.bfloat16), down_new.astype(jnp.bfloat16).reshape(up_new.shape)]
    )
    low_bits = replicas.bit_length() - 1
    holding = gather_group(piece, replicas)
    ordering = jnp.bitwise_xor(jnp.arange(replicas, dtype=jnp.int32), owner % replicas)
    holding = jnp.take(holding, ordering, axis=0)
    model_width = tokens.shape[2]
    up_serve = holding[:, 0].reshape(model_width, up_new.shape[1])
    down_serve = holding[:, 1].reshape(replicas * down_new.shape[0], down_new.shape[1])
    rows_dev = tokens.shape[1]
    slot_count = rows_dev // replicas
    decoded = []
    for step_index in range(tokens.shape[0]):
        chosen = routes[step_index]
        matches = chosen[:, :, None] == jnp.bitwise_xor(labels, owner // replicas)
        gates = jnp.sum(jnp.where(matches, mix_weights[step_index][:, :, None], 0.0), axis=1)
        routed = jnp.any(matches, axis=1)
        outgoing = jnp.where(
            routed.T[:, :, None], tokens[step_index][None], jnp.zeros((), jnp.bfloat16)
        )
        outgoing = outgoing.reshape(peer_count, slot_count, model_width)
        received = lax.all_to_all(outgoing, "expert", split_axis=0, concat_axis=0, tiled=True)
        flat_rows = received.reshape(-1, model_width)
        hidden = jax.nn.silu(
            jnp.dot(flat_rows, up_serve, preferred_element_type=jnp.float32)
        ).astype(jnp.bfloat16)
        all_units = lax.all_gather(hidden, "dp", axis=1, tiled=True)
        produced = jnp.dot(all_units, down_serve, preferred_element_type=jnp.float32).astype(
            jnp.bfloat16
        )
        produced = produced.reshape(received.shape[0], received.shape[1], produced.shape[1])
        returned = lax.all_to_all(produced, "expert", split_axis=0, concat_axis=0, tiled=True)
        returned = returned.reshape(EXPERTS, rows_dev, returned.shape[2])
        mixed = jnp.einsum("re,erd->rd", gates, returned.astype(jnp.float32))
        decoded.append(mixed.astype(jnp.bfloat16))
    return (up_update[None], down_update[None], jnp.stack(decoded))


def solution(mesh):
    return jax.shard_map(
        per_device,
        mesh=mesh,
        in_specs=(
            P(None, "expert", None),
            P(None, "expert", None),
            P(None, "expert", None),
            P("dp", "expert", None, None),
            P("dp", "expert", None, None),
            P("expert", None, "dp"),
            P("expert", None, "dp"),
            P("expert", None, "dp"),
            P("expert", None, "dp"),
            P("expert", None, "dp"),
            P("expert", None, "dp"),
            P("dp", None),
            P(),
        ),
        out_specs=(P("expert", None, "dp"), P("expert", None, "dp"), P(None, "expert", "dp")),
        check_vma=False,
    )
```

```python
import functools

import jax
import jax.numpy as jnp
from jax import lax
from jax.experimental import pallas as pl
from jax.experimental.pallas import tpu as pltpu
from jax.sharding import PartitionSpec as P

EXPERTS = 4
LINES = 4
CORES = 2

beta_one = 0.9
beta_two = 0.95
first_fix = 1.0 - 0.9**10
second_fix = 1.0 - 0.95**10
epsilon = 1e-08
weight_decay = 0.1
learn_rate = 0.001


def adamw_step(gradient, weight, first, second):
    first_new = beta_one * first + (1.0 - beta_one) * gradient
    second_new = beta_two * second + (1.0 - beta_two) * gradient * gradient
    update = (
        first_new / first_fix / (jnp.sqrt(second_new / second_fix) + epsilon)
        + weight_decay * weight
    )
    return (update, weight - learn_rate * update)


class Copies:
    def __init__(self, send, recv):
        self.send, self.recv, self.used, self.open = send, recv, 0, []

    def make(self, src, dst, device):
        copy = pltpu.make_async_remote_copy(
            src_ref=src,
            dst_ref=dst,
            send_sem=self.send.at[self.used],
            recv_sem=self.recv.at[self.used],
            device_id=device,
            device_id_type=pl.DeviceIdType.MESH,
        )
        self.used += 1
        self.open.append(copy)
        return copy


def kernel(
    sizes,
    key_ref,
    tokens,
    gates,
    counts,
    up_partial,
    down_partial,
    up_master,
    down_master,
    up_first,
    down_first,
    up_second,
    down_second,
    up_update,
    down_update,
    decoded,
    slabs,
    tok_out,
    tok_in,
    gates_in,
    counts_in,
    up_pair,
    down_pair,
    up_out,
    down_out,
    up_in,
    down_in,
    up_all,
    down_all,
    partial_units,
    swap_out,
    swap_in,
    unit_blocks,
    units_out,
    units_in,
    units_all,
    units_flat,
    back_out,
    back_in,
    send_sems,
    recv_sems,
):
    planes, lines, chips, group, rows, slab, width, units, columns = sizes
    dp_size = chips * CORES
    place = lax.axis_index("expert")
    z, y = place // lines, place % lines
    dp = lax.axis_index("dp")
    x, core = dp // CORES, dp % CORES
    key = key_ref[0]
    key_line = key % lines
    key_plane = key // lines % group
    key_group = key // (lines * group)

    def at_plane(step):
        return ((z + step + planes) % planes * lines + y, dp)

    def at_line(step):
        return (z * lines + (y + step) % lines, dp)

    def at_dp(other):
        return (place, other)

    twin = dp + 1 - 2 * core
    lane = lax.broadcasted_iota(jnp.int32, (rows, 2 * units), 1)
    low = lane < units

    def turn(value):
        return pltpu.roll(value, units, value.ndim - 1)

    partners = (
        [at_plane(1), at_plane(-1)]
        + [at_line(k) for k in range(1, lines)]
        + [at_dp((dp + k) % dp_size) for k in range(1, dp_size)]
    )
    barrier = pltpu.get_barrier_semaphore()
    for partner in partners:
        pl.semaphore_signal(
            barrier, inc=1, device_id=partner, device_id_type=pl.DeviceIdType.MESH
        )
    pl.semaphore_wait(barrier, len(partners))

    copies = Copies(send_sems, recv_sems)

    up_swap, down_swap = [], []
    for chip in range(chips):
        column = pl.multiple_of((chip * CORES + 1 - core) * width, width)
        copy = copies.make(up_partial.at[:, pl.ds(column, width)], up_pair.at[chip], at_dp(twin))
        copy.start()
        up_swap.append(copy)
    counts_moves = []
    for k in range(1, dp_size):
        copy = copies.make(counts, counts_in.at[k], at_dp((dp + k) % dp_size))
        copy.start()
        counts_moves.append(copy)
    for chip in range(chips):
        column = pl.multiple_of((chip * CORES + 1 - core) * columns, columns)
        copy = copies.make(
            down_partial.at[:, pl.ds(column, columns)], down_pair.at[chip], at_dp(twin)
        )
        copy.start()
        down_swap.append(copy)

    for s in range(group * lines):
        slabs[s] = tokens[:, s * slab : (s + 1) * slab]
    for line in range(lines):
        for plane in range(group):
            which = jnp.bitwise_xor(plane, key_plane) * lines + jnp.bitwise_xor(line, key_line)
            tok_out[line, plane] = slabs[which]
    token_moves = []
    for k in range(1, lines):
        copy = copies.make(tok_out.at[(y + k) % lines], tok_in.at[y], at_line(k))
        copy.start()
        token_moves.append(copy)
        copy = copies.make(gates, gates_in.at[y], at_line(k))
        copy.start()
        token_moves.append(copy)
    tok_in[y] = tok_out[y]
    gates_in[y] = gates[...]

    up_moves, down_moves = [], []

    def pair_sum(partial, pair, chip, extent):
        column = pl.multiple_of((chip * CORES + core) * extent, extent)
        return partial[:, pl.ds(column, extent)].astype(jnp.float32) + pair[chip].astype(
            jnp.float32
        )

    for copy in up_swap:
        copy.wait_recv()
    for k in range(1, chips):
        chip = (x + k) % chips
        up_out[k] = pair_sum(up_partial, up_pair, chip, width).astype(jnp.bfloat16)
        copy = copies.make(up_out.at[k], up_in.at[k], at_dp(chip * CORES + core))
        copy.start()
        up_moves.append(copy)
    for copy in down_swap:
        copy.wait_recv()
    for k in range(1, chips):
        chip = (x + k) % chips
        down_out[k] = pair_sum(down_partial, down_pair, chip, columns).astype(jnp.bfloat16)
        copy = copies.make(down_out.at[k], down_in.at[k], at_dp(chip * CORES + core))
        copy.start()
        down_moves.append(copy)

    for copy in counts_moves:
        copy.wait_recv()
    totals = counts[...].astype(jnp.float32)
    for k in range(1, dp_size):
        totals = totals + counts_in[k].astype(jnp.float32)
    owner = jnp.bitwise_xor(z // group, key_group)
    label = lax.broadcasted_iota(jnp.int32, totals.shape, 1)
    row_count = jnp.sum(jnp.where(label == owner, totals, 0.0))

    up_total = pair_sum(up_partial, up_pair, x, width)
    for copy in up_moves:
        copy.wait_recv()
    for k in range(1, chips):
        up_total = up_total + up_in[k].astype(jnp.float32)
    update, new = adamw_step(up_total / row_count, up_master[...], up_first[...], up_second[...])
    up_update[...] = update
    up_all[z] = new.astype(jnp.bfloat16)

    farthest = planes // 2

    def ring(blocks, extent):
        half = extent // 2
        steps = {}
        for step in range(1, farthest + 1):
            steps[step] = []
            for way, part in ((1, 0), (-1, 1), (1, 1), (-1, 0)):
                if step == farthest and (way == 1) != (part == 0):
                    continue
                block = (z - way * (step - 1) + planes) % planes
                ref = blocks.at[block, pl.ds(part * half, half)]
                steps[step].append(copies.make(ref, ref, at_plane(way)))
        return steps

    def send(steps, step):
        for copy in steps[step]:
            copy.start()

    def pass_on(steps, step):
        onward = steps.get(step + 1, [])
        for at, copy in enumerate(steps[step]):
            copy.wait_recv()
            if at < len(onward):
                onward[at].start()

    up_ring = ring(up_all, slab)
    down_ring = ring(down_all, units)

    def meet(block):
        held = tok_in[:, block % group].reshape(lines * rows, slab)
        product = jnp.dot(held, up_all[block], preferred_element_type=jnp.float32)
        partial_units[block // group] = partial_units[block // group] + product

    def meet_step(step):
        meet((z - step + planes) % planes)
        if step < farthest:
            meet((z + step) % planes)

    send(up_ring, 1)
    partial_units[...] = jnp.zeros_like(partial_units)

    down_total = pair_sum(down_partial, down_pair, x, columns)
    for copy in down_moves:
        copy.wait_recv()
    for k in range(1, chips):
        down_total = down_total + down_in[k].astype(jnp.float32)
    update, new = adamw_step(
        down_total / row_count, down_master[...], down_first[...], down_second[...]
    )
    down_update[...] = update
    down_all[z] = new.astype(jnp.bfloat16)

    for copy in token_moves:
        copy.wait_recv()
    pass_on(up_ring, 1)
    meet(z)
    meet_step(1)
    for step in range(2, farthest - 1):
        pass_on(up_ring, step)
        meet_step(step)
    send(down_ring, 1)
    pass_on(up_ring, farthest - 1)
    meet_step(farthest - 1)
    pass_on(up_ring, farthest)
    meet_step(farthest)

    half = lines * rows // 2
    swap_out[...] = partial_units[:, pl.ds(pl.multiple_of((1 - core) * half, half), half)].astype(
        jnp.bfloat16
    )
    swap = copies.make(swap_out, swap_in, at_dp(twin))
    swap.start()
    pass_on(down_ring, 1)
    swap.wait_recv()

    def blocks_of(value, first):
        upper, lower = value[:, :rows], value[:, rows:]
        unit_blocks[first] = jnp.where(low, upper, turn(lower))
        unit_blocks[first + 1] = jnp.where(low, turn(upper), lower)

    blocks_of(partial_units[:, pl.ds(pl.multiple_of(core * half, half), half)], 2 * core)
    blocks_of(swap_in[...].astype(jnp.float32), 2 * (1 - core))
    unit_moves = []
    for k in range(1, lines):
        line = (y + k) % lines
        units_out[k] = unit_blocks[jnp.bitwise_xor(line, key_line)].astype(jnp.bfloat16)
        copy = copies.make(units_out.at[k], units_in.at[k], at_line(k))
        copy.start()
        unit_moves.append(copy)
    pass_on(down_ring, 2)
    summed = unit_blocks[jnp.bitwise_xor(y, key_line)]
    for copy in unit_moves:
        copy.wait_recv()
    for k in range(1, lines):
        summed = summed + units_in[k].astype(jnp.float32)
    for g in range(EXPERTS):
        upper = gates_in[2 * core][:, g : g + 1]
        lower = gates_in[2 * core + 1][:, g : g + 1]
        gate = jnp.where(low, upper, lower)
        units_all[dp, g] = (jax.nn.silu(summed[g]) * gate).astype(jnp.bfloat16)
    spread = []
    for k in range(1, dp_size):
        copy = copies.make(units_all.at[dp], units_all.at[dp], at_dp((dp + k) % dp_size))
        copy.start()
        spread.append(copy)
    for step in range(3, farthest - 1):
        pass_on(down_ring, step)
    for copy in spread:
        copy.wait_recv()

    for g in range(EXPERTS):
        for pair in range(group // 2):
            column = (g * group + 2 * pair) * units
            for owner_core in range(CORES):
                even = units_all[
                    jnp.bitwise_xor(2 * pair, key_plane) * CORES + owner_core, g
                ].astype(jnp.float32)
                odd = units_all[
                    jnp.bitwise_xor(2 * pair + 1, key_plane) * CORES + owner_core, g
                ].astype(jnp.float32)
                row = owner_core * half
                units_flat[row : row + rows, column : column + 2 * units] = jnp.where(
                    low, even, turn(odd)
                ).astype(jnp.bfloat16)
                units_flat[row + rows : row + half, column : column + 2 * units] = jnp.where(
                    low, turn(even), odd
                ).astype(jnp.bfloat16)
    for step in range(farthest - 1, farthest + 1):
        pass_on(down_ring, step)

    flat_down = down_all[...].reshape(planes * units, columns)

    def produce(line):
        held = units_flat[pl.ds(pl.multiple_of(line * rows, rows), rows)]
        return jnp.dot(held, flat_down, preferred_element_type=jnp.float32)

    back_moves = []
    for k in range(1, lines):
        back_out[k] = produce((y + k) % lines).astype(jnp.bfloat16)
        copy = copies.make(back_out.at[k], back_in.at[k], at_line(k))
        copy.start()
        back_moves.append(copy)
    result = produce(y)
    for copy in back_moves:
        copy.wait_recv()
    for k in range(1, lines):
        result = result + back_in[k].astype(jnp.float32)
    decoded[...] = result.astype(jnp.bfloat16)

    for copy in copies.open:
        copy.wait_send()


def per_device(
    tokens,
    routes,
    mix_weights,
    up_partial,
    down_partial,
    up_master,
    down_master,
    up_first,
    down_first,
    up_second,
    down_second,
    counts,
    owner_key,
):
    planes = lax.axis_size("expert") // LINES
    dp_size = lax.axis_size("dp")
    chips = dp_size // CORES
    group = planes // EXPERTS
    steps, rows_dev, model = tokens.shape
    rows = steps * rows_dev
    slab, width = up_master.shape[1:]
    units, columns = down_master.shape[1:]
    bf16, f32 = jnp.bfloat16, jnp.float32

    holder = jnp.bitwise_xor(
        jnp.arange(EXPERTS, dtype=jnp.int32), owner_key[0] // (LINES * group)
    )
    matches = routes[..., None] == holder
    gates = jnp.sum(jnp.where(matches, mix_weights[..., None], 0.0), axis=2)
    gates = jnp.pad(gates.reshape(rows, EXPERTS), ((0, 0), (0, 128 - EXPERTS)))
    counts = jnp.pad(counts, ((0, 7), (0, 128 - EXPERTS)))

    copies = (
        2 * chips
        + (dp_size - 1)
        + 2 * (LINES - 1)
        + 2 * (chips - 1)
        + 2 * 2 * (planes - 1)
        + 1
        + (LINES - 1)
        + (dp_size - 1)
        + (LINES - 1)
    )
    scratch = [
        pltpu.VMEM((group * LINES, rows, slab), bf16),
        pltpu.VMEM((LINES, group, rows, slab), bf16),
        pltpu.VMEM((LINES, group, rows, slab), bf16),
        pltpu.VMEM((LINES, rows, 128), f32),
        pltpu.VMEM((dp_size, 8, 128), jnp.int32),
        pltpu.VMEM((chips, slab, width), bf16),
        pltpu.VMEM((chips, units, columns), bf16),
        pltpu.VMEM((chips, slab, width), bf16),
        pltpu.VMEM((chips, units, columns), bf16),
        pltpu.VMEM((chips, slab, width), bf16),
        pltpu.VMEM((chips, units, columns), bf16),
        pltpu.VMEM((planes, slab, width), bf16),
        pltpu.VMEM((planes, units, columns), bf16),
        pltpu.VMEM((EXPERTS, LINES * rows, width), f32),
        pltpu.VMEM((EXPERTS, LINES * rows // 2, width), bf16),
        pltpu.VMEM((EXPERTS, LINES * rows // 2, width), bf16),
        pltpu.VMEM((LINES, EXPERTS, rows, 2 * units), f32),
        pltpu.VMEM((LINES, EXPERTS, rows, 2 * units), bf16),
        pltpu.VMEM((LINES, EXPERTS, rows, 2 * units), bf16),
        pltpu.VMEM((dp_size, EXPERTS, rows, 2 * units), bf16),
        pltpu.VMEM((LINES * rows, planes * units), bf16),
        pltpu.VMEM((LINES, rows, columns), bf16),
        pltpu.VMEM((LINES, rows, columns), bf16),
        pltpu.SemaphoreType.DMA((copies,)),
        pltpu.SemaphoreType.DMA((copies,)),
    ]
    vmem = pl.BlockSpec(memory_space=pltpu.VMEM)
    sizes = (planes, LINES, chips, group, rows, slab, width, units, columns)
    up_update, down_update, decoded = pl.pallas_call(
        functools.partial(kernel, sizes),
        out_shape=(
            jax.ShapeDtypeStruct((slab, width), f32),
            jax.ShapeDtypeStruct((units, columns), f32),
            jax.ShapeDtypeStruct((rows, columns), bf16),
        ),
        in_specs=[pl.BlockSpec(memory_space=pltpu.SMEM)] + [vmem] * 11,
        out_specs=(vmem, vmem, vmem),
        scratch_shapes=scratch,
        compiler_params=pltpu.CompilerParams(
            collective_id=0, has_side_effects=True, vmem_limit_bytes=48 * 1024 * 1024
        ),
        cost_estimate=pl.CostEstimate(
            flops=2 * 2 * LINES * rows * planes * slab * width,
            bytes_accessed=6 * 1024 * 1024,
            transcendentals=0,
        ),
    )(
        owner_key,
        tokens.reshape(rows, model),
        gates,
        counts,
        up_partial[0, 0],
        down_partial[0, 0],
        up_master[0],
        down_master[0],
        up_first[0],
        down_first[0],
        up_second[0],
        down_second[0],
    )
    return (up_update[None], down_update[None], decoded.reshape(steps, rows_dev, columns))


def solution(mesh):
    return jax.shard_map(
        per_device,
        mesh=mesh,
        in_specs=(
            P(None, "expert", None),
            P(None, "expert", None),
            P(None, "expert", None),
            P("dp", "expert", None, None),
            P("dp", "expert", None, None),
            P("expert", None, "dp"),
            P("expert", None, "dp"),
            P("expert", None, "dp"),
            P("expert", None, "dp"),
            P("expert", None, "dp"),
            P("expert", None, "dp"),
            P("dp", None),
            P(),
        ),
        out_specs=(P("expert", None, "dp"), P("expert", None, "dp"), P(None, "expert", "dp")),
        check_vma=False,
    )
```

```python
import functools

import jax
import jax.numpy as jnp
from jax import lax
from jax.experimental import pallas as pl
from jax.experimental.pallas import tpu as pltpu
from jax.sharding import PartitionSpec as P

EXPERTS = 4
LINES = 4
CORES = 2

beta_one = 0.9
beta_two = 0.95
first_fix = 1.0 - 0.9**10
second_fix = 1.0 - 0.95**10
epsilon = 1e-08
weight_decay = 0.1
learn_rate = 0.001


def adamw_step(gradient, weight, first, second):
    first_new = beta_one * first + (1.0 - beta_one) * gradient
    second_new = beta_two * second + (1.0 - beta_two) * gradient * gradient
    update = (
        first_new / first_fix / (jnp.sqrt(second_new / second_fix) + epsilon)
        + weight_decay * weight
    )
    return (update, weight - learn_rate * update)


class Copy:
    def __init__(self, copy):
        self.copy, self.started, self.landed = copy, False, False

    def start(self):
        self.copy.start()
        self.started = True

    def wait_recv(self):
        self.copy.wait_recv()
        self.landed = True


class Copies:
    def __init__(self, send, recv):
        self.send, self.recv, self.made = send, recv, []

    def make(self, src, dst, device):
        at = len(self.made)
        copy = Copy(
            pltpu.make_async_remote_copy(
                src_ref=src,
                dst_ref=dst,
                send_sem=self.send.at[at],
                recv_sem=self.recv.at[at],
                device_id=device,
                device_id_type=pl.DeviceIdType.MESH,
            )
        )
        self.made.append(copy)
        return copy

    def drain(self):
        for copy in self.made:
            if copy.started:
                copy.copy.wait_send()
                if not copy.landed:
                    copy.copy.wait_recv()


def kernel(
    sizes,
    key_ref,
    gates,
    counts,
    tokens_far,
    up_partial,
    down_partial,
    up_master_far,
    down_master_far,
    up_first_far,
    down_first_far,
    up_second_far,
    down_second_far,
    up_update_far,
    down_update_far,
    decoded_far,
    tokens,
    up_own,
    down_own,
    up_master,
    down_master,
    up_first,
    down_first,
    up_second,
    down_second,
    up_update,
    down_update,
    decoded,
    slabs,
    tok_out,
    tok_in,
    gates_in,
    counts_in,
    up_pair,
    down_pair,
    up_out,
    down_out,
    up_in,
    down_in,
    up_all,
    down_all,
    partial_units,
    swap_out,
    swap_in,
    unit_blocks,
    units_out,
    units_in,
    units_all,
    units_flat,
    back_out,
    back_in,
    send_sems,
    recv_sems,
    local_sems,
):
    planes, lines, chips, group, rows, slab, width, units, columns = sizes
    dp_size = chips * CORES
    place = lax.axis_index("expert")
    z, y = place // lines, place % lines
    dp = lax.axis_index("dp")
    x, core = dp // CORES, dp % CORES
    key = key_ref[0]
    key_line = key % lines
    key_plane = key // lines % group
    key_group = key // (lines * group)

    def at_plane(step):
        return ((z + step + planes) % planes * lines + y, dp)

    def at_line(step):
        return (z * lines + (y + step) % lines, dp)

    def at_dp(other):
        return (place, other)

    twin = dp + 1 - 2 * core
    lane = lax.broadcasted_iota(jnp.int32, (rows, 2 * units), 1)
    low = lane < units

    def turn(value):
        return pltpu.roll(value, units, value.ndim - 1)

    def local(src, dst, at):
        copy = pltpu.make_async_copy(src, dst, local_sems.at[at])
        copy.start()
        return copy

    tokens_load = local(tokens_far, tokens, 0)
    up_loads, down_loads = [], []
    for chip in range(chips):
        column = pl.multiple_of((chip * CORES + core) * width, width)
        up_loads.append(local(up_partial.at[:, pl.ds(column, width)], up_own.at[chip], 1 + chip))
    for chip in range(chips):
        column = pl.multiple_of((chip * CORES + core) * columns, columns)
        down_loads.append(
            local(down_partial.at[:, pl.ds(column, columns)], down_own.at[chip], 1 + chips + chip)
        )
    base = 1 + 2 * chips
    up_loads += [
        local(up_master_far, up_master, base),
        local(up_first_far, up_first, base + 1),
        local(up_second_far, up_second, base + 2),
    ]
    down_loads += [
        local(down_master_far, down_master, base + 3),
        local(down_first_far, down_first, base + 4),
        local(down_second_far, down_second, base + 5),
    ]
    base += 6

    partners = (
        [at_plane(1), at_plane(-1)]
        + [at_line(k) for k in range(1, lines)]
        + [at_dp((dp + k) % dp_size) for k in range(1, dp_size)]
    )
    barrier = pltpu.get_barrier_semaphore()
    for partner in partners:
        pl.semaphore_signal(
            barrier, inc=1, device_id=partner, device_id_type=pl.DeviceIdType.MESH
        )
    pl.semaphore_wait(barrier, len(partners))

    copies = Copies(send_sems, recv_sems)

    up_swap, down_swap = [], []
    for chip in range(chips):
        column = pl.multiple_of((chip * CORES + 1 - core) * width, width)
        copy = copies.make(up_partial.at[:, pl.ds(column, width)], up_pair.at[chip], at_dp(twin))
        copy.start()
        up_swap.append(copy)
    counts_moves = []
    for k in range(1, dp_size):
        copy = copies.make(counts, counts_in.at[k], at_dp((dp + k) % dp_size))
        copy.start()
        counts_moves.append(copy)
    for chip in range(chips):
        column = pl.multiple_of((chip * CORES + 1 - core) * columns, columns)
        copy = copies.make(
            down_partial.at[:, pl.ds(column, columns)], down_pair.at[chip], at_dp(twin)
        )
        copy.start()
        down_swap.append(copy)

    tokens_load.wait()
    for s in range(group * lines):
        slabs[s] = tokens[:, s * slab : (s + 1) * slab]
    for line in range(lines):
        for plane in range(group):
            which = jnp.bitwise_xor(plane, key_plane) * lines + jnp.bitwise_xor(line, key_line)
            tok_out[line, plane] = slabs[which]
    token_moves = []
    for k in range(1, lines):
        copy = copies.make(tok_out.at[(y + k) % lines], tok_in.at[y], at_line(k))
        copy.start()
        token_moves.append(copy)
        copy = copies.make(gates, gates_in.at[y], at_line(k))
        copy.start()
        token_moves.append(copy)
    tok_in[y] = tok_out[y]
    gates_in[y] = gates[...]

    up_moves, down_moves = [], []

    def pair_sum(own, pair, chip):
        return own[chip].astype(jnp.float32) + pair[chip].astype(jnp.float32)

    for copy in up_loads:
        copy.wait()
    for copy in up_swap:
        copy.wait_recv()
    for k in range(1, chips):
        chip = (x + k) % chips
        up_out[k] = pair_sum(up_own, up_pair, chip).astype(jnp.bfloat16)
        copy = copies.make(up_out.at[k], up_in.at[k], at_dp(chip * CORES + core))
        copy.start()
        up_moves.append(copy)
    for copy in down_loads:
        copy.wait()
    for copy in down_swap:
        copy.wait_recv()
    for k in range(1, chips):
        chip = (x + k) % chips
        down_out[k] = pair_sum(down_own, down_pair, chip).astype(jnp.bfloat16)
        copy = copies.make(down_out.at[k], down_in.at[k], at_dp(chip * CORES + core))
        copy.start()
        down_moves.append(copy)

    for copy in counts_moves:
        copy.wait_recv()
    totals = counts[...].astype(jnp.float32)
    for k in range(1, dp_size):
        totals = totals + counts_in[k].astype(jnp.float32)
    owner = jnp.bitwise_xor(z // group, key_group)
    label = lax.broadcasted_iota(jnp.int32, totals.shape, 1)
    row_count = jnp.sum(jnp.where(label == owner, totals, 0.0))

    up_total = pair_sum(up_own, up_pair, x)
    for copy in up_moves:
        copy.wait_recv()
    for k in range(1, chips):
        up_total = up_total + up_in[k].astype(jnp.float32)
    update, new = adamw_step(up_total / row_count, up_master[...], up_first[...], up_second[...])
    up_update[...] = update
    up_all[z] = new.astype(jnp.bfloat16)

    farthest = planes // 2

    def ring(blocks, extent):
        half = extent // 2
        steps = {}
        for step in range(1, farthest + 1):
            steps[step] = []
            for way, part in ((1, 0), (-1, 1), (1, 1), (-1, 0)):
                if step == farthest and (way == 1) != (part == 0):
                    continue
                block = (z - way * (step - 1) + planes) % planes
                ref = blocks.at[block, pl.ds(part * half, half)]
                steps[step].append(copies.make(ref, ref, at_plane(way)))
        return steps

    def send(steps, step):
        for copy in steps[step]:
            copy.start()

    def pass_on(steps, step):
        onward = steps.get(step + 1, [])
        for at, copy in enumerate(steps[step]):
            copy.wait_recv()
            if at < len(onward):
                onward[at].start()

    up_ring = ring(up_all, slab)
    down_ring = ring(down_all, units)

    def meet(block):
        held = tok_in[:, block % group].reshape(lines * rows, slab)
        product = jnp.dot(held, up_all[block], preferred_element_type=jnp.float32)
        partial_units[block // group] = partial_units[block // group] + product

    def meet_step(step):
        meet((z - step + planes) % planes)
        if step < farthest:
            meet((z + step) % planes)

    send(up_ring, 1)
    writes = [local(up_update, up_update_far, base)]
    partial_units[...] = jnp.zeros_like(partial_units)

    down_total = pair_sum(down_own, down_pair, x)
    for copy in down_moves:
        copy.wait_recv()
    for k in range(1, chips):
        down_total = down_total + down_in[k].astype(jnp.float32)
    update, new = adamw_step(
        down_total / row_count, down_master[...], down_first[...], down_second[...]
    )
    down_update[...] = update
    writes.append(local(down_update, down_update_far, base + 1))
    down_all[z] = new.astype(jnp.bfloat16)

    for copy in token_moves:
        copy.wait_recv()
    pass_on(up_ring, 1)
    meet(z)
    meet_step(1)
    for step in range(2, farthest - 1):
        pass_on(up_ring, step)
        meet_step(step)
    send(down_ring, 1)
    pass_on(up_ring, farthest - 1)
    meet_step(farthest - 1)
    pass_on(up_ring, farthest)
    meet_step(farthest)

    half = lines * rows // 2
    swap_out[...] = partial_units[:, pl.ds(pl.multiple_of((1 - core) * half, half), half)].astype(
        jnp.bfloat16
    )
    swap = copies.make(swap_out, swap_in, at_dp(twin))
    swap.start()
    pass_on(down_ring, 1)
    swap.wait_recv()

    def blocks_of(value, first):
        upper, lower = value[:, :rows], value[:, rows:]
        unit_blocks[first] = jnp.where(low, upper, turn(lower))
        unit_blocks[first + 1] = jnp.where(low, turn(upper), lower)

    blocks_of(partial_units[:, pl.ds(pl.multiple_of(core * half, half), half)], 2 * core)
    blocks_of(swap_in[...].astype(jnp.float32), 2 * (1 - core))
    unit_moves = []
    for k in range(1, lines):
        line = (y + k) % lines
        units_out[k] = unit_blocks[jnp.bitwise_xor(line, key_line)].astype(jnp.bfloat16)
        copy = copies.make(units_out.at[k], units_in.at[k], at_line(k))
        copy.start()
        unit_moves.append(copy)
    pass_on(down_ring, 2)
    summed = unit_blocks[jnp.bitwise_xor(y, key_line)]
    for copy in unit_moves:
        copy.wait_recv()
    for k in range(1, lines):
        summed = summed + units_in[k].astype(jnp.float32)
    for g in range(EXPERTS):
        upper = gates_in[2 * core][:, g : g + 1]
        lower = gates_in[2 * core + 1][:, g : g + 1]
        gate = jnp.where(low, upper, lower)
        units_all[dp, g] = (jax.nn.silu(summed[g]) * gate).astype(jnp.bfloat16)
    spread = []
    for k in range(1, dp_size):
        copy = copies.make(units_all.at[dp], units_all.at[dp], at_dp((dp + k) % dp_size))
        copy.start()
        spread.append(copy)
    for step in range(3, farthest - 1):
        pass_on(down_ring, step)
    for copy in spread:
        copy.wait_recv()

    for g in range(EXPERTS):
        for pair in range(group // 2):
            column = (g * group + 2 * pair) * units
            for owner_core in range(CORES):
                even = units_all[
                    jnp.bitwise_xor(2 * pair, key_plane) * CORES + owner_core, g
                ].astype(jnp.float32)
                odd = units_all[
                    jnp.bitwise_xor(2 * pair + 1, key_plane) * CORES + owner_core, g
                ].astype(jnp.float32)
                row = owner_core * half
                units_flat[row : row + rows, column : column + 2 * units] = jnp.where(
                    low, even, turn(odd)
                ).astype(jnp.bfloat16)
                units_flat[row + rows : row + half, column : column + 2 * units] = jnp.where(
                    low, turn(even), odd
                ).astype(jnp.bfloat16)
    for step in range(farthest - 1, farthest + 1):
        pass_on(down_ring, step)

    flat_down = down_all[...].reshape(planes * units, columns)

    def produce(line):
        held = units_flat[pl.ds(pl.multiple_of(line * rows, rows), rows)]
        return jnp.dot(held, flat_down, preferred_element_type=jnp.float32)

    back_moves = []
    for k in range(1, lines):
        back_out[k] = produce((y + k) % lines).astype(jnp.bfloat16)
        copy = copies.make(back_out.at[k], back_in.at[k], at_line(k))
        copy.start()
        back_moves.append(copy)
    result = produce(y)
    for copy in back_moves:
        copy.wait_recv()
    for k in range(1, lines):
        result = result + back_in[k].astype(jnp.float32)
    decoded[...] = result.astype(jnp.bfloat16)
    writes.append(local(decoded, decoded_far, base + 2))
    for copy in writes:
        copy.wait()

    copies.drain()


def per_device(
    tokens,
    routes,
    mix_weights,
    up_partial,
    down_partial,
    up_master,
    down_master,
    up_first,
    down_first,
    up_second,
    down_second,
    counts,
    owner_key,
):
    planes = lax.axis_size("expert") // LINES
    dp_size = lax.axis_size("dp")
    chips = dp_size // CORES
    group = planes // EXPERTS
    steps, rows_dev, model = tokens.shape
    rows = steps * rows_dev
    slab, width = up_master.shape[1:]
    units, columns = down_master.shape[1:]
    bf16, f32 = jnp.bfloat16, jnp.float32

    holder = jnp.bitwise_xor(
        jnp.arange(EXPERTS, dtype=jnp.int32), owner_key[0] // (LINES * group)
    )
    matches = routes[..., None] == holder
    gates = jnp.sum(jnp.where(matches, mix_weights[..., None], 0.0), axis=2)
    gates = jnp.pad(gates.reshape(rows, EXPERTS), ((0, 0), (0, 128 - EXPERTS)))
    counts = jnp.pad(counts, ((0, 7), (0, 128 - EXPERTS)))

    copies = (
        2 * chips
        + (dp_size - 1)
        + 2 * (LINES - 1)
        + 2 * (chips - 1)
        + 2 * 2 * (planes - 1)
        + 1
        + (LINES - 1)
        + (dp_size - 1)
        + (LINES - 1)
    )
    scratch = [
        pltpu.VMEM((rows, model), bf16),
        pltpu.VMEM((chips, slab, width), bf16),
        pltpu.VMEM((chips, units, columns), bf16),
    ]
    for _ in range(4):
        scratch += [pltpu.VMEM((slab, width), f32), pltpu.VMEM((units, columns), f32)]
    scratch += [
        pltpu.VMEM((rows, columns), bf16),
        pltpu.VMEM((group * LINES, rows, slab), bf16),
        pltpu.VMEM((LINES, group, rows, slab), bf16),
        pltpu.VMEM((LINES, group, rows, slab), bf16),
        pltpu.VMEM((LINES, rows, 128), f32),
        pltpu.VMEM((dp_size, 8, 128), jnp.int32),
        pltpu.VMEM((chips, slab, width), bf16),
        pltpu.VMEM((chips, units, columns), bf16),
        pltpu.VMEM((chips, slab, width), bf16),
        pltpu.VMEM((chips, units, columns), bf16),
        pltpu.VMEM((chips, slab, width), bf16),
        pltpu.VMEM((chips, units, columns), bf16),
        pltpu.VMEM((planes, slab, width), bf16),
        pltpu.VMEM((planes, units, columns), bf16),
        pltpu.VMEM((EXPERTS, LINES * rows, width), f32),
        pltpu.VMEM((EXPERTS, LINES * rows // 2, width), bf16),
        pltpu.VMEM((EXPERTS, LINES * rows // 2, width), bf16),
        pltpu.VMEM((LINES, EXPERTS, rows, 2 * units), f32),
        pltpu.VMEM((LINES, EXPERTS, rows, 2 * units), bf16),
        pltpu.VMEM((LINES, EXPERTS, rows, 2 * units), bf16),
        pltpu.VMEM((dp_size, EXPERTS, rows, 2 * units), bf16),
        pltpu.VMEM((LINES * rows, planes * units), bf16),
        pltpu.VMEM((LINES, rows, columns), bf16),
        pltpu.VMEM((LINES, rows, columns), bf16),
        pltpu.SemaphoreType.DMA((copies,)),
        pltpu.SemaphoreType.DMA((copies,)),
        pltpu.SemaphoreType.DMA((2 * chips + 10,)),
    ]
    vmem = pl.BlockSpec(memory_space=pltpu.VMEM)
    hbm = pl.BlockSpec(memory_space=pltpu.HBM)
    sizes = (planes, LINES, chips, group, rows, slab, width, units, columns)
    up_update, down_update, decoded = pl.pallas_call(
        functools.partial(kernel, sizes),
        out_shape=(
            jax.ShapeDtypeStruct((slab, width), f32),
            jax.ShapeDtypeStruct((units, columns), f32),
            jax.ShapeDtypeStruct((rows, columns), bf16),
        ),
        in_specs=[pl.BlockSpec(memory_space=pltpu.SMEM), vmem, vmem] + [hbm] * 9,
        out_specs=(hbm, hbm, hbm),
        scratch_shapes=scratch,
        compiler_params=pltpu.CompilerParams(
            collective_id=0, has_side_effects=True, vmem_limit_bytes=64 * 1024 * 1024
        ),
        cost_estimate=pl.CostEstimate(
            flops=2 * 2 * LINES * rows * planes * slab * width,
            bytes_accessed=6 * 1024 * 1024,
            transcendentals=0,
        ),
    )(
        owner_key,
        gates,
        counts,
        tokens.reshape(rows, model),
        up_partial[0, 0],
        down_partial[0, 0],
        up_master[0],
        down_master[0],
        up_first[0],
        down_first[0],
        up_second[0],
        down_second[0],
    )
    return (up_update[None], down_update[None], decoded.reshape(steps, rows_dev, columns))


def solution(mesh):
    return jax.shard_map(
        per_device,
        mesh=mesh,
        in_specs=(
            P(None, "expert", None),
            P(None, "expert", None),
            P(None, "expert", None),
            P("dp", "expert", None, None),
            P("dp", "expert", None, None),
            P("expert", None, "dp"),
            P("expert", None, "dp"),
            P("expert", None, "dp"),
            P("expert", None, "dp"),
            P("expert", None, "dp"),
            P("expert", None, "dp"),
            P("dp", None),
            P(),
        ),
        out_specs=(P("expert", None, "dp"), P("expert", None, "dp"), P(None, "expert", "dp")),
        check_vma=False,
    )
```

```python
import functools

import jax
import jax.numpy as jnp
from jax import lax
from jax.experimental import pallas as pl
from jax.experimental.pallas import tpu as pltpu
from jax.sharding import PartitionSpec as P

EXPERTS = 4
LINES = 4
CORES = 2

beta_one = 0.9
beta_two = 0.95
first_fix = 1.0 - 0.9**10
second_fix = 1.0 - 0.95**10
epsilon = 1e-08
weight_decay = 0.1
learn_rate = 0.001


def adamw_step(gradient, weight, first, second):
    first_new = beta_one * first + (1.0 - beta_one) * gradient
    second_new = beta_two * second + (1.0 - beta_two) * gradient * gradient
    update = (
        first_new / first_fix / (jnp.sqrt(second_new / second_fix) + epsilon)
        + weight_decay * weight
    )
    return (update, weight - learn_rate * update)


class Copy:
    def __init__(self, copy):
        self.copy, self.started, self.landed = copy, False, False

    def start(self):
        self.copy.start()
        self.started = True

    def wait_recv(self):
        self.copy.wait_recv()
        self.landed = True


class Copies:
    def __init__(self, send, recv):
        self.send, self.recv, self.made = send, recv, []

    def make(self, src, dst, device):
        at = len(self.made)
        copy = Copy(
            pltpu.make_async_remote_copy(
                src_ref=src,
                dst_ref=dst,
                send_sem=self.send.at[at],
                recv_sem=self.recv.at[at],
                device_id=device,
                device_id_type=pl.DeviceIdType.MESH,
            )
        )
        self.made.append(copy)
        return copy

    def drain(self):
        for copy in self.made:
            if copy.started:
                copy.copy.wait_send()
                if not copy.landed:
                    copy.copy.wait_recv()


def kernel(
    sizes,
    key_ref,
    gates,
    counts,
    tokens_far,
    up_partial,
    down_partial,
    up_master_far,
    down_master_far,
    up_first_far,
    down_first_far,
    up_second_far,
    down_second_far,
    up_update_far,
    down_update_far,
    decoded_far,
    tokens,
    up_own,
    down_own,
    up_master,
    down_master,
    up_first,
    down_first,
    up_second,
    down_second,
    up_update,
    down_update,
    decoded,
    slabs,
    tok_out,
    tok_in,
    gates_in,
    counts_in,
    up_pair,
    down_pair,
    up_out,
    down_out,
    up_in,
    down_in,
    up_all,
    down_all,
    partial_units,
    swap_out,
    swap_in,
    unit_blocks,
    units_out,
    units_in,
    units_all,
    units_flat,
    back_sum,
    back_out,
    back_in,
    send_sems,
    recv_sems,
    local_sems,
):
    planes, lines, chips, group, rows, slab, width, units, columns = sizes
    dp_size = chips * CORES
    place = lax.axis_index("expert")
    z, y = place // lines, place % lines
    dp = lax.axis_index("dp")
    x, core = dp // CORES, dp % CORES
    key = key_ref[0]
    key_line = key % lines
    key_plane = key // lines % group
    key_group = key // (lines * group)

    def at_plane(step):
        return ((z + step + planes) % planes * lines + y, dp)

    def at_line(step):
        return (z * lines + (y + step) % lines, dp)

    def at_dp(other):
        return (place, other)

    twin = dp + 1 - 2 * core
    lane = lax.broadcasted_iota(jnp.int32, (rows, 2 * units), 1)
    low = lane < units

    def turn(value):
        return pltpu.roll(value, units, value.ndim - 1)

    def local(src, dst, at):
        copy = pltpu.make_async_copy(src, dst, local_sems.at[at])
        copy.start()
        return copy

    tokens_load = local(tokens_far, tokens, 0)
    up_loads, down_loads = [], []
    for chip in range(chips):
        column = pl.multiple_of((chip * CORES + core) * width, width)
        up_loads.append(local(up_partial.at[:, pl.ds(column, width)], up_own.at[chip], 1 + chip))
    for chip in range(chips):
        column = pl.multiple_of((chip * CORES + core) * columns, columns)
        down_loads.append(
            local(down_partial.at[:, pl.ds(column, columns)], down_own.at[chip], 1 + chips + chip)
        )
    base = 1 + 2 * chips
    up_loads += [
        local(up_master_far, up_master, base),
        local(up_first_far, up_first, base + 1),
        local(up_second_far, up_second, base + 2),
    ]
    down_loads += [
        local(down_master_far, down_master, base + 3),
        local(down_first_far, down_first, base + 4),
        local(down_second_far, down_second, base + 5),
    ]
    base += 6

    partners = (
        [at_plane(1), at_plane(-1)]
        + [at_line(k) for k in range(1, lines)]
        + [at_dp((dp + k) % dp_size) for k in range(1, dp_size)]
    )
    barrier = pltpu.get_barrier_semaphore()
    for partner in partners:
        pl.semaphore_signal(
            barrier, inc=1, device_id=partner, device_id_type=pl.DeviceIdType.MESH
        )
    pl.semaphore_wait(barrier, len(partners))

    copies = Copies(send_sems, recv_sems)

    halves = [pl.ds(part * (slab // 2), slab // 2) for part in range(2)]
    up_swap, down_swap = [[], []], []
    for part in range(2):
        for chip in range(chips):
            column = pl.multiple_of((chip * CORES + 1 - core) * width, width)
            copy = copies.make(
                up_partial.at[halves[part], pl.ds(column, width)],
                up_pair.at[chip, halves[part]],
                at_dp(twin),
            )
            copy.start()
            up_swap[part].append(copy)
    counts_moves = []
    for k in range(1, dp_size):
        copy = copies.make(counts, counts_in.at[k], at_dp((dp + k) % dp_size))
        copy.start()
        counts_moves.append(copy)
    for chip in range(chips):
        column = pl.multiple_of((chip * CORES + 1 - core) * columns, columns)
        copy = copies.make(
            down_partial.at[:, pl.ds(column, columns)], down_pair.at[chip], at_dp(twin)
        )
        copy.start()
        down_swap.append(copy)

    up_moves, down_moves = [[], []], []
    for copy in up_loads[:chips]:
        copy.wait()
    for part in range(2):
        for copy in up_swap[part]:
            copy.wait_recv()
        for k in range(1, chips):
            chip = (x + k) % chips
            total = up_own[chip, halves[part]].astype(jnp.float32) + up_pair[
                chip, halves[part]
            ].astype(jnp.float32)
            up_out[k, halves[part]] = total.astype(jnp.bfloat16)
            copy = copies.make(
                up_out.at[k, halves[part]], up_in.at[k, halves[part]], at_dp(chip * CORES + core)
            )
            copy.start()
            up_moves[part].append(copy)

    tokens_load.wait()
    for s in range(group * lines):
        slabs[s] = tokens[:, s * slab : (s + 1) * slab]
    for line in range(lines):
        for plane in range(group):
            which = jnp.bitwise_xor(plane, key_plane) * lines + jnp.bitwise_xor(line, key_line)
            tok_out[line, plane] = slabs[which]
    share = pl.ds(pl.multiple_of(core * (rows // 2), rows // 2), rows // 2)
    token_moves, gate_moves = [], []
    for k in range(1, lines):
        copy = copies.make(tok_out.at[(y + k) % lines, :, share], tok_in.at[y, :, share], at_line(k))
        copy.start()
        token_moves.append(copy)
        copy = copies.make(gates, gates_in.at[y], at_line(k))
        copy.start()
        gate_moves.append(copy)
    tok_in[y] = tok_out[y]
    gates_in[y] = gates[...]

    farthest = planes // 2

    def ring(blocks, parts):
        steps = []
        for step in range(1, farthest + 1):
            made = {}
            for at, (row, column, last_way) in enumerate(parts):
                for way in (1, -1):
                    if step == farthest and way != last_way:
                        continue
                    block = (z - way * (step - 1) + planes) % planes
                    ref = blocks.at[block, row, column]
                    made[at, way] = copies.make(ref, ref, at_plane(way))
            steps.append(made)
        return steps

    def send(steps, parts):
        for (at, _), copy in steps[0].items():
            if at in parts:
                copy.start()

    def pass_on(steps, step):
        onward = steps[step] if step < farthest else {}
        for place_of, copy in steps[step - 1].items():
            copy.wait_recv()
            if place_of in onward:
                onward[place_of].start()

    quarter = slab // 4
    whole = pl.ds(0, width)
    up_ring = ring(
        up_all,
        [(pl.ds(at * quarter, quarter), whole, 1 if at % 2 == 0 else -1) for at in range(4)],
    )
    left = columns - columns // 256 * 128
    sides = [(0, left), (left, columns - left)]
    down_rings = [
        ring(
            down_all,
            [
                (pl.ds(at * (units // 2), units // 2), pl.ds(low_column, extent), 1 - 2 * at)
                for at in range(2)
            ],
        )
        for low_column, extent in sides
    ]

    for copy in counts_moves:
        copy.wait_recv()
    totals = counts[...].astype(jnp.float32)
    for k in range(1, dp_size):
        totals = totals + counts_in[k].astype(jnp.float32)
    owner = jnp.bitwise_xor(z // group, key_group)
    label = lax.broadcasted_iota(jnp.int32, totals.shape, 1)
    row_count = jnp.sum(jnp.where(label == owner, totals, 0.0))
    for copy in up_loads[chips:]:
        copy.wait()
    for part in range(2):
        half = halves[part]
        total = up_own[x, half].astype(jnp.float32) + up_pair[x, half].astype(jnp.float32)
        for copy in up_moves[part]:
            copy.wait_recv()
        for k in range(1, chips):
            total = total + up_in[k, half].astype(jnp.float32)
        update, new = adamw_step(total / row_count, up_master[half], up_first[half], up_second[half])
        up_update[half] = update
        up_all[z, half] = new.astype(jnp.bfloat16)
        send(up_ring, (2 * part, 2 * part + 1))
        if part == 0:
            for copy in down_loads:
                copy.wait()
            for copy in down_swap:
                copy.wait_recv()
            for k in range(1, chips):
                chip = (x + k) % chips
                total = down_own[chip].astype(jnp.float32) + down_pair[chip].astype(jnp.float32)
                down_out[k] = total.astype(jnp.bfloat16)
                copy = copies.make(down_out.at[k], down_in.at[k], at_dp(chip * CORES + core))
                copy.start()
                down_moves.append(copy)
    writes = [local(up_update, up_update_far, base)]

    pass_on(up_ring, 1)
    total = down_own[x].astype(jnp.float32) + down_pair[x].astype(jnp.float32)
    for copy in down_moves:
        copy.wait_recv()
    for k in range(1, chips):
        total = total + down_in[k].astype(jnp.float32)
    update, new = adamw_step(total / row_count, down_master[...], down_first[...], down_second[...])
    down_update[...] = update
    down_all[z] = new.astype(jnp.bfloat16)
    writes.append(local(down_update, down_update_far, base + 1))
    partial_units[...] = jnp.zeros_like(partial_units)
    pass_on(up_ring, 2)
    twin_moves = []
    for k in range(1, lines):
        token_moves[k - 1].wait_recv()
        gate_moves[k - 1].wait_recv()
        held = tok_in.at[(y - k + lines) % lines, :, share]
        copy = copies.make(held, held, at_dp(twin))
        copy.start()
        twin_moves.append(copy)

    def meet(block):
        held = tok_in[:, block % group].reshape(lines * rows, slab)
        product = jnp.dot(held, up_all[block], preferred_element_type=jnp.float32)
        partial_units[block // group] = partial_units[block // group] + product

    def meet_step(step):
        meet((z - step + planes) % planes)
        if step < farthest:
            meet((z + step) % planes)

    def down_pass(first, second):
        if first:
            pass_on(down_rings[0], first)
        if second:
            pass_on(down_rings[1], second)

    pass_on(up_ring, 3)
    send(down_rings[0], (0, 1))
    for copy in twin_moves:
        copy.wait_recv()
    meet(z)
    meet_step(1)
    pass_on(up_ring, 4)
    send(down_rings[1], (0, 1))
    meet_step(2)
    meet_step(3)
    for step in range(5, farthest):
        down_pass(step - 4, step - 5)
        pass_on(up_ring, step)
        meet_step(step - 1)
    meet_step(farthest - 1)
    down_pass(farthest - 4, farthest - 5)
    pass_on(up_ring, farthest)
    meet_step(farthest)

    half = lines * rows // 2
    swap_out[...] = partial_units[:, pl.ds(pl.multiple_of((1 - core) * half, half), half)].astype(
        jnp.bfloat16
    )
    swap = copies.make(swap_out, swap_in, at_dp(twin))
    swap.start()

    def blocks_of(value, first):
        upper, lower = value[:, :rows], value[:, rows:]
        unit_blocks[first] = jnp.where(low, upper, turn(lower))
        unit_blocks[first + 1] = jnp.where(low, turn(upper), lower)

    blocks_of(partial_units[:, pl.ds(pl.multiple_of(core * half, half), half)], 2 * core)
    swap.wait_recv()
    blocks_of(swap_in[...].astype(jnp.float32), 2 * (1 - core))
    unit_moves = []
    for k in range(1, lines):
        line = (y + k) % lines
        units_out[k] = unit_blocks[jnp.bitwise_xor(line, key_line)].astype(jnp.bfloat16)
        copy = copies.make(units_out.at[k], units_in.at[k], at_line(k))
        copy.start()
        unit_moves.append(copy)
    down_pass(farthest - 3, farthest - 4)
    summed = unit_blocks[jnp.bitwise_xor(y, key_line)]
    for copy in unit_moves:
        copy.wait_recv()
    for k in range(1, lines):
        summed = summed + units_in[k].astype(jnp.float32)
    for g in range(EXPERTS):
        upper = gates_in[2 * core][:, g : g + 1]
        lower = gates_in[2 * core + 1][:, g : g + 1]
        gate = jnp.where(low, upper, lower)
        units_all[dp, g] = (jax.nn.silu(summed[g]) * gate).astype(jnp.bfloat16)
    spread = []
    for k in range(1, chips):
        copy = copies.make(
            units_all.at[dp], units_all.at[dp], at_dp((x + k) % chips * CORES + core)
        )
        copy.start()
        spread.append(copy)
    copy = copies.make(units_all.at[dp], units_all.at[dp], at_dp(twin))
    copy.start()
    twin_moves = [copy]
    down_pass(farthest - 2, farthest - 3)
    for k in range(1, chips):
        spread[k - 1].wait_recv()
        held = units_all.at[(x - k + chips) % chips * CORES + core]
        copy = copies.make(held, held, at_dp(twin))
        copy.start()
        twin_moves.append(copy)
    down_pass(farthest - 1, farthest - 2)
    for copy in twin_moves:
        copy.wait_recv()

    for g in range(EXPERTS):
        for pair in range(group // 2):
            column = (g * group + 2 * pair) * units
            for owner_core in range(CORES):
                even = units_all[
                    jnp.bitwise_xor(2 * pair, key_plane) * CORES + owner_core, g
                ].astype(jnp.float32)
                odd = units_all[
                    jnp.bitwise_xor(2 * pair + 1, key_plane) * CORES + owner_core, g
                ].astype(jnp.float32)
                row = owner_core * half
                units_flat[row : row + rows, column : column + 2 * units] = jnp.where(
                    low, even, turn(odd)
                ).astype(jnp.bfloat16)
                units_flat[row + rows : row + half, column : column + 2 * units] = jnp.where(
                    low, turn(even), odd
                ).astype(jnp.bfloat16)

    back_moves = []
    for side, (low_column, extent) in enumerate(sides):
        if side == 0:
            down_pass(farthest, farthest - 1)
        else:
            down_pass(0, farthest)
        side_columns = pl.ds(low_column, extent)
        product = jnp.dot(
            units_flat[...],
            down_all[:, :, side_columns].reshape(planes * units, extent),
            preferred_element_type=jnp.float32,
        ).reshape(lines, rows, extent)
        back_sum[:, :, side_columns] = product
        back_out[:, :, side_columns] = product.astype(jnp.bfloat16)
        for k in range(1, lines):
            copy = copies.make(
                back_out.at[(y + k) % lines, :, side_columns],
                back_in.at[k, :, side_columns],
                at_line(k),
            )
            copy.start()
            back_moves.append(copy)
    result = back_sum[y]
    for copy in back_moves:
        copy.wait_recv()
    for k in range(1, lines):
        result = result + back_in[k].astype(jnp.float32)
    decoded[...] = result.astype(jnp.bfloat16)
    writes.append(local(decoded, decoded_far, base + 2))
    for copy in writes:
        copy.wait()

    copies.drain()


def per_device(
    tokens,
    routes,
    mix_weights,
    up_partial,
    down_partial,
    up_master,
    down_master,
    up_first,
    down_first,
    up_second,
    down_second,
    counts,
    owner_key,
):
    planes = lax.axis_size("expert") // LINES
    dp_size = lax.axis_size("dp")
    chips = dp_size // CORES
    group = planes // EXPERTS
    steps, rows_dev, model = tokens.shape
    rows = steps * rows_dev
    slab, width = up_master.shape[1:]
    units, columns = down_master.shape[1:]
    bf16, f32 = jnp.bfloat16, jnp.float32

    holder = jnp.bitwise_xor(
        jnp.arange(EXPERTS, dtype=jnp.int32), owner_key[0] // (LINES * group)
    )
    matches = routes[..., None] == holder
    gates = jnp.sum(jnp.where(matches, mix_weights[..., None], 0.0), axis=2)
    gates = jnp.pad(gates.reshape(rows, EXPERTS), ((0, 0), (0, 128 - EXPERTS)))
    counts = jnp.pad(counts, ((0, 7), (0, 128 - EXPERTS)))

    copies = (
        3 * chips
        + (dp_size - 1)
        + 3 * (LINES - 1)
        + 3 * (chips - 1)
        + (4 + 2 + 2) * (planes - 1)
        + 1
        + (LINES - 1)
        + 2 * chips - 1
        + 2 * (LINES - 1)
    )
    scratch = [
        pltpu.VMEM((rows, model), bf16),
        pltpu.VMEM((chips, slab, width), bf16),
        pltpu.VMEM((chips, units, columns), bf16),
    ]
    for _ in range(4):
        scratch += [pltpu.VMEM((slab, width), f32), pltpu.VMEM((units, columns), f32)]
    scratch += [
        pltpu.VMEM((rows, columns), bf16),
        pltpu.VMEM((group * LINES, rows, slab), bf16),
        pltpu.VMEM((LINES, group, rows, slab), bf16),
        pltpu.VMEM((LINES, group, rows, slab), bf16),
        pltpu.VMEM((LINES, rows, 128), f32),
        pltpu.VMEM((dp_size, 8, 128), jnp.int32),
        pltpu.VMEM((chips, slab, width), bf16),
        pltpu.VMEM((chips, units, columns), bf16),
        pltpu.VMEM((chips, slab, width), bf16),
        pltpu.VMEM((chips, units, columns), bf16),
        pltpu.VMEM((chips, slab, width), bf16),
        pltpu.VMEM((chips, units, columns), bf16),
        pltpu.VMEM((planes, slab, width), bf16),
        pltpu.VMEM((planes, units, columns), bf16),
        pltpu.VMEM((EXPERTS, LINES * rows, width), f32),
        pltpu.VMEM((EXPERTS, LINES * rows // 2, width), bf16),
        pltpu.VMEM((EXPERTS, LINES * rows // 2, width), bf16),
        pltpu.VMEM((LINES, EXPERTS, rows, 2 * units), f32),
        pltpu.VMEM((LINES, EXPERTS, rows, 2 * units), bf16),
        pltpu.VMEM((LINES, EXPERTS, rows, 2 * units), bf16),
        pltpu.VMEM((dp_size, EXPERTS, rows, 2 * units), bf16),
        pltpu.VMEM((LINES * rows, planes * units), bf16),
        pltpu.VMEM((LINES, rows, columns), f32),
        pltpu.VMEM((LINES, rows, columns), bf16),
        pltpu.VMEM((LINES, rows, columns), bf16),
        pltpu.SemaphoreType.DMA((copies,)),
        pltpu.SemaphoreType.DMA((copies,)),
        pltpu.SemaphoreType.DMA((2 * chips + 10,)),
    ]
    vmem = pl.BlockSpec(memory_space=pltpu.VMEM)
    hbm = pl.BlockSpec(memory_space=pltpu.HBM)
    sizes = (planes, LINES, chips, group, rows, slab, width, units, columns)
    up_update, down_update, decoded = pl.pallas_call(
        functools.partial(kernel, sizes),
        out_shape=(
            jax.ShapeDtypeStruct((slab, width), f32),
            jax.ShapeDtypeStruct((units, columns), f32),
            jax.ShapeDtypeStruct((rows, columns), bf16),
        ),
        in_specs=[pl.BlockSpec(memory_space=pltpu.SMEM), vmem, vmem] + [hbm] * 9,
        out_specs=(hbm, hbm, hbm),
        scratch_shapes=scratch,
        compiler_params=pltpu.CompilerParams(
            collective_id=0, has_side_effects=True, vmem_limit_bytes=64 * 1024 * 1024
        ),
        cost_estimate=pl.CostEstimate(
            flops=2 * 2 * LINES * rows * planes * slab * width,
            bytes_accessed=6 * 1024 * 1024,
            transcendentals=0,
        ),
    )(
        owner_key,
        gates,
        counts,
        tokens.reshape(rows, model),
        up_partial[0, 0],
        down_partial[0, 0],
        up_master[0],
        down_master[0],
        up_first[0],
        down_first[0],
        up_second[0],
        down_second[0],
    )
    return (up_update[None], down_update[None], decoded.reshape(steps, rows_dev, columns))


def solution(mesh):
    return jax.shard_map(
        per_device,
        mesh=mesh,
        in_specs=(
            P(None, "expert", None),
            P(None, "expert", None),
            P(None, "expert", None),
            P("dp", "expert", None, None),
            P("dp", "expert", None, None),
            P("expert", None, "dp"),
            P("expert", None, "dp"),
            P("expert", None, "dp"),
            P("expert", None, "dp"),
            P("expert", None, "dp"),
            P("expert", None, "dp"),
            P("dp", None),
            P(),
        ),
        out_specs=(P("expert", None, "dp"), P("expert", None, "dp"), P(None, "expert", "dp")),
        check_vma=False,
    )
```

```python
import functools

import jax
import jax.numpy as jnp
from jax import lax
from jax.experimental import pallas as pl
from jax.experimental.pallas import tpu as pltpu
from jax.sharding import PartitionSpec as P

EXPERTS = 4
LINES = 4
CORES = 2

beta_one = 0.9
beta_two = 0.95
first_fix = 1.0 - 0.9**10
second_fix = 1.0 - 0.95**10
epsilon = 1e-08
weight_decay = 0.1
learn_rate = 0.001


def adamw_step(gradient, weight, first, second):
    first_new = beta_one * first + (1.0 - beta_one) * gradient
    second_new = beta_two * second + (1.0 - beta_two) * gradient * gradient
    update = (
        first_new / first_fix / (jnp.sqrt(second_new / second_fix) + epsilon)
        + weight_decay * weight
    )
    return (update, weight - learn_rate * update)


class Copy:
    def __init__(self, copy):
        self.copy, self.started, self.landed = copy, False, False

    def start(self):
        self.copy.start()
        self.started = True

    def wait_recv(self):
        self.copy.wait_recv()
        self.landed = True


class Copies:
    def __init__(self, send, recv):
        self.send, self.recv, self.made = send, recv, []

    def make(self, src, dst, device):
        at = len(self.made)
        copy = Copy(
            pltpu.make_async_remote_copy(
                src_ref=src,
                dst_ref=dst,
                send_sem=self.send.at[at],
                recv_sem=self.recv.at[at],
                device_id=device,
                device_id_type=pl.DeviceIdType.MESH,
            )
        )
        self.made.append(copy)
        return copy

    def drain(self):
        for copy in self.made:
            if copy.started:
                copy.copy.wait_send()
                if not copy.landed:
                    copy.copy.wait_recv()


def kernel(
    sizes,
    key_ref,
    routes,
    mix_weights,
    own_counts,
    tokens_far,
    up_partial,
    down_partial,
    up_master_far,
    down_master_far,
    up_first_far,
    down_first_far,
    up_second_far,
    down_second_far,
    up_update_far,
    down_update_far,
    decoded_far,
    tokens,
    up_own,
    down_own,
    up_master,
    down_master,
    up_first,
    down_first,
    up_second,
    down_second,
    up_update,
    down_update,
    decoded,
    slabs,
    tok_out,
    tok_in,
    gates,
    gates_in,
    counts,
    counts_in,
    up_pair,
    down_pair,
    up_out,
    down_out,
    up_in,
    down_in,
    up_all,
    down_all,
    partial_units,
    swap_out,
    swap_in,
    unit_blocks,
    units_out,
    units_in,
    units_all,
    units_flat,
    back_sum,
    back_out,
    back_in,
    send_sems,
    recv_sems,
    local_sems,
):
    planes, lines, chips, group, rows, slab, width, units, columns = sizes
    dp_size = chips * CORES
    place = lax.axis_index("expert")
    z, y = place // lines, place % lines
    dp = lax.axis_index("dp")
    x, core = dp // CORES, dp % CORES
    key = key_ref[0]
    key_line = key % lines
    key_plane = key // lines % group
    key_group = key // (lines * group)

    def at_plane(step):
        return ((z + step + planes) % planes * lines + y, dp)

    def at_line(step):
        return (z * lines + (y + step) % lines, dp)

    def at_dp(other):
        return (place, other)

    twin = dp + 1 - 2 * core
    lane = lax.broadcasted_iota(jnp.int32, (rows, 2 * units), 1)
    low = lane < units

    def turn(value):
        return pltpu.roll(value, units, value.ndim - 1)

    partners = (
        [at_plane(1), at_plane(-1)]
        + [at_line(k) for k in range(1, lines)]
        + [at_dp((dp + k) % dp_size) for k in range(1, dp_size)]
    )
    barrier = pltpu.get_barrier_semaphore()
    for partner in partners:
        pl.semaphore_signal(
            barrier, inc=1, device_id=partner, device_id_type=pl.DeviceIdType.MESH
        )

    def local(src, dst, at):
        copy = pltpu.make_async_copy(src, dst, local_sems.at[at])
        copy.start()
        return copy

    up_load = local(up_partial, up_own, 0)
    pl.semaphore_wait(barrier, len(partners))

    copies = Copies(send_sems, recv_sems)

    halves = [pl.ds(part * (slab // 2), slab // 2) for part in range(2)]
    up_swap, down_swap = [[], []], []
    for part in range(2):
        for chip in range(chips):
            column = pl.multiple_of((chip * CORES + 1 - core) * width, width)
            copy = copies.make(
                up_partial.at[halves[part], pl.ds(column, width)],
                up_pair.at[chip, halves[part]],
                at_dp(twin),
            )
            copy.start()
            up_swap[part].append(copy)

    up_moves, down_moves = [[], []], []

    def up_sum(chip, part):
        column = pl.multiple_of((chip * CORES + core) * width, width)
        return up_own[halves[part], pl.ds(column, width)].astype(jnp.float32) + up_pair[
            chip, halves[part]
        ].astype(jnp.float32)

    def down_sum(chip):
        column = pl.multiple_of((chip * CORES + core) * columns, columns)
        return down_own[:, pl.ds(column, columns)].astype(jnp.float32) + down_pair[chip].astype(
            jnp.float32
        )

    up_load.wait()
    for part in range(2):
        for copy in up_swap[part]:
            copy.wait_recv()
        for k in range(1, chips):
            chip = (x + k) % chips
            up_out[k, halves[part]] = up_sum(chip, part).astype(jnp.bfloat16)
            copy = copies.make(
                up_out.at[k, halves[part]], up_in.at[k, halves[part]], at_dp(chip * CORES + core)
            )
            copy.start()
            up_moves[part].append(copy)

    tokens_load = local(tokens_far, tokens, 1)
    up_loads = [
        local(up_master_far, up_master, 2),
        local(up_first_far, up_first, 3),
        local(up_second_far, up_second, 4),
    ]
    counts[...] = jnp.zeros_like(counts)
    counts[0:1, 0:EXPERTS] = own_counts[...]
    counts_moves = []
    for k in range(1, dp_size):
        copy = copies.make(counts, counts_in.at[k], at_dp((dp + k) % dp_size))
        copy.start()
        counts_moves.append(copy)
    for chip in range(chips):
        column = pl.multiple_of((chip * CORES + 1 - core) * columns, columns)
        copy = copies.make(
            down_partial.at[:, pl.ds(column, columns)], down_pair.at[chip], at_dp(twin)
        )
        copy.start()
        down_swap.append(copy)
    down_loads = [
        local(down_partial, down_own, 5),
        local(down_master_far, down_master, 6),
        local(down_first_far, down_first, 7),
        local(down_second_far, down_second, 8),
    ]
    base = 9

    gates[...] = jnp.zeros_like(gates)
    for g in range(EXPERTS):
        chosen = routes[...] == jnp.bitwise_xor(g, key_group)
        gate = jnp.sum(jnp.where(chosen, mix_weights[...], 0.0), axis=1)
        for step in range(gate.shape[0]):
            extent = gate.shape[1]
            gates[g : g + 1, step * extent : (step + 1) * extent] = gate[step : step + 1]

    tokens_load.wait()
    for s in range(group * lines):
        slabs[s] = tokens[:, s * slab : (s + 1) * slab]
    for line in range(lines):
        for plane in range(group):
            which = jnp.bitwise_xor(plane, key_plane) * lines + jnp.bitwise_xor(line, key_line)
            tok_out[line, plane] = slabs[which]
    share = pl.ds(pl.multiple_of(core * (rows // 2), rows // 2), rows // 2)
    token_moves, gate_moves = [], []
    for k in range(1, lines):
        copy = copies.make(tok_out.at[(y + k) % lines, :, share], tok_in.at[y, :, share], at_line(k))
        copy.start()
        token_moves.append(copy)
        copy = copies.make(gates, gates_in.at[y], at_line(k))
        copy.start()
        gate_moves.append(copy)
    tok_in[y] = tok_out[y]
    gates_in[y] = gates[...]

    farthest = planes // 2

    def ring(blocks, parts):
        steps = []
        for step in range(1, farthest + 1):
            made = {}
            for at, (row, column, last_way) in enumerate(parts):
                for way in (1, -1):
                    if step == farthest and way != last_way:
                        continue
                    block = (z - way * (step - 1) + planes) % planes
                    ref = blocks.at[block, row, column]
                    made[at, way] = copies.make(ref, ref, at_plane(way))
            steps.append(made)
        return steps

    def send(steps, parts):
        for (at, _), copy in steps[0].items():
            if at in parts:
                copy.start()

    def pass_on(steps, step):
        onward = steps[step] if step < farthest else {}
        for place_of, copy in steps[step - 1].items():
            copy.wait_recv()
            if place_of in onward:
                onward[place_of].start()

    quarter = slab // 4
    whole = pl.ds(0, width)
    up_ring = ring(
        up_all,
        [(pl.ds(at * quarter, quarter), whole, 1 if at % 2 == 0 else -1) for at in range(4)],
    )
    left = columns - columns // 256 * 128
    sides = [(0, left), (left, columns - left)]
    down_rings = [
        ring(
            down_all,
            [
                (pl.ds(at * (units // 2), units // 2), pl.ds(low_column, extent), 1 - 2 * at)
                for at in range(2)
            ],
        )
        for low_column, extent in sides
    ]

    for copy in counts_moves:
        copy.wait_recv()
    totals = counts[...].astype(jnp.float32)
    for k in range(1, dp_size):
        totals = totals + counts_in[k].astype(jnp.float32)
    owner = jnp.bitwise_xor(z // group, key_group)
    label = lax.broadcasted_iota(jnp.int32, totals.shape, 1)
    row_count = jnp.sum(jnp.where(label == owner, totals, 0.0))
    for copy in up_loads:
        copy.wait()
    for part in range(2):
        half = halves[part]
        total = up_sum(x, part)
        for copy in up_moves[part]:
            copy.wait_recv()
        for k in range(1, chips):
            total = total + up_in[k, half].astype(jnp.float32)
        update, new = adamw_step(total / row_count, up_master[half], up_first[half], up_second[half])
        up_update[half] = update
        up_all[z, half] = new.astype(jnp.bfloat16)
        send(up_ring, (2 * part, 2 * part + 1))
        if part == 0:
            for copy in down_loads:
                copy.wait()
            for copy in down_swap:
                copy.wait_recv()
            for k in range(1, chips):
                chip = (x + k) % chips
                down_out[k] = down_sum(chip).astype(jnp.bfloat16)
                copy = copies.make(down_out.at[k], down_in.at[k], at_dp(chip * CORES + core))
                copy.start()
                down_moves.append(copy)
    writes = [local(up_update, up_update_far, base)]

    pass_on(up_ring, 1)
    total = down_sum(x)
    for copy in down_moves:
        copy.wait_recv()
    for k in range(1, chips):
        total = total + down_in[k].astype(jnp.float32)
    update, new = adamw_step(total / row_count, down_master[...], down_first[...], down_second[...])
    down_update[...] = update
    down_all[z] = new.astype(jnp.bfloat16)
    writes.append(local(down_update, down_update_far, base + 1))
    partial_units[...] = jnp.zeros_like(partial_units)
    pass_on(up_ring, 2)
    twin_moves = []
    for k in range(1, lines):
        token_moves[k - 1].wait_recv()
        gate_moves[k - 1].wait_recv()
        held = tok_in.at[(y - k + lines) % lines, :, share]
        copy = copies.make(held, held, at_dp(twin))
        copy.start()
        twin_moves.append(copy)

    def meet(block):
        held = tok_in[:, block % group].reshape(lines * rows, slab)
        product = jnp.dot(held, up_all[block], preferred_element_type=jnp.float32)
        partial_units[block // group] = partial_units[block // group] + product

    def meet_step(step):
        meet((z - step + planes) % planes)
        if step < farthest:
            meet((z + step) % planes)

    def down_pass(first, second):
        if first:
            pass_on(down_rings[0], first)
        if second:
            pass_on(down_rings[1], second)

    pass_on(up_ring, 3)
    send(down_rings[0], (0, 1))
    for copy in twin_moves:
        copy.wait_recv()
    meet(z)
    meet_step(1)
    pass_on(up_ring, 4)
    send(down_rings[1], (0, 1))
    meet_step(2)
    meet_step(3)
    for step in range(5, farthest):
        down_pass(step - 4, step - 5)
        pass_on(up_ring, step)
        meet_step(step - 1)
    meet_step(farthest - 1)
    down_pass(farthest - 4, farthest - 5)
    pass_on(up_ring, farthest)
    meet_step(farthest)

    half = lines * rows // 2
    swap_out[...] = partial_units[:, pl.ds(pl.multiple_of((1 - core) * half, half), half)].astype(
        jnp.bfloat16
    )
    swap = copies.make(swap_out, swap_in, at_dp(twin))
    swap.start()

    def blocks_of(value, first):
        upper, lower = value[:, :rows], value[:, rows:]
        unit_blocks[first] = jnp.where(low, upper, turn(lower))
        unit_blocks[first + 1] = jnp.where(low, turn(upper), lower)

    blocks_of(partial_units[:, pl.ds(pl.multiple_of(core * half, half), half)], 2 * core)
    swap.wait_recv()
    blocks_of(swap_in[...].astype(jnp.float32), 2 * (1 - core))
    unit_moves = []
    for k in range(1, lines):
        line = (y + k) % lines
        units_out[k] = unit_blocks[jnp.bitwise_xor(line, key_line)].astype(jnp.bfloat16)
        copy = copies.make(units_out.at[k], units_in.at[k], at_line(k))
        copy.start()
        unit_moves.append(copy)
    down_pass(farthest - 3, farthest - 4)
    summed = unit_blocks[jnp.bitwise_xor(y, key_line)]
    for copy in unit_moves:
        copy.wait_recv()
    for k in range(1, lines):
        summed = summed + units_in[k].astype(jnp.float32)
    upper, lower = gates_in[2 * core].T, gates_in[2 * core + 1].T
    for g in range(EXPERTS):
        gate = jnp.where(low, upper[:rows, g : g + 1], lower[:rows, g : g + 1])
        units_all[dp, g] = (jax.nn.silu(summed[g]) * gate).astype(jnp.bfloat16)
    spread = []
    for k in range(1, chips):
        copy = copies.make(
            units_all.at[dp], units_all.at[dp], at_dp((x + k) % chips * CORES + core)
        )
        copy.start()
        spread.append(copy)
    copy = copies.make(units_all.at[dp], units_all.at[dp], at_dp(twin))
    copy.start()
    twin_moves = [copy]
    down_pass(farthest - 2, farthest - 3)
    for k in range(1, chips):
        spread[k - 1].wait_recv()
        held = units_all.at[(x - k + chips) % chips * CORES + core]
        copy = copies.make(held, held, at_dp(twin))
        copy.start()
        twin_moves.append(copy)
    down_pass(farthest - 1, farthest - 2)
    for copy in twin_moves:
        copy.wait_recv()

    for g in range(EXPERTS):
        for pair in range(group // 2):
            column = (g * group + 2 * pair) * units
            for owner_core in range(CORES):
                even = units_all[
                    jnp.bitwise_xor(2 * pair, key_plane) * CORES + owner_core, g
                ].astype(jnp.float32)
                odd = units_all[
                    jnp.bitwise_xor(2 * pair + 1, key_plane) * CORES + owner_core, g
                ].astype(jnp.float32)
                row = owner_core * half
                units_flat[row : row + rows, column : column + 2 * units] = jnp.where(
                    low, even, turn(odd)
                ).astype(jnp.bfloat16)
                units_flat[row + rows : row + half, column : column + 2 * units] = jnp.where(
                    low, turn(even), odd
                ).astype(jnp.bfloat16)

    back_moves = []
    for side, (low_column, extent) in enumerate(sides):
        if side == 0:
            down_pass(farthest, farthest - 1)
        else:
            down_pass(0, farthest)
        side_columns = pl.ds(low_column, extent)
        product = jnp.dot(
            units_flat[...],
            down_all[:, :, side_columns].reshape(planes * units, extent),
            preferred_element_type=jnp.float32,
        ).reshape(lines, rows, extent)
        back_sum[:, :, side_columns] = product
        back_out[:, :, side_columns] = product.astype(jnp.bfloat16)
        for k in range(1, lines):
            copy = copies.make(
                back_out.at[(y + k) % lines, :, side_columns],
                back_in.at[k, :, side_columns],
                at_line(k),
            )
            copy.start()
            back_moves.append(copy)
    result = back_sum[y]
    for copy in back_moves:
        copy.wait_recv()
    for k in range(1, lines):
        result = result + back_in[k].astype(jnp.float32)
    decoded[...] = result.astype(jnp.bfloat16)
    writes.append(local(decoded, decoded_far, base + 2))
    for copy in writes:
        copy.wait()

    copies.drain()


def hand_out(a, b, c, a_out, b_out, c_out, a_held, b_held, c_held, sems):
    held = (a_held, b_held, c_held)
    reads = [
        pltpu.make_async_copy(src, dst, sems.at[at])
        for at, (src, dst) in enumerate(zip((a, b, c), held))
    ]
    writes = [
        pltpu.make_async_copy(src, dst, sems.at[3 + at])
        for at, (src, dst) in enumerate(zip(held, (a_out, b_out, c_out)))
    ]
    for copy in reads:
        copy.start()
    for read, write in zip(reads, writes):
        read.wait()
        write.start()
    for copy in writes:
        copy.wait()


def per_device(
    tokens,
    routes,
    mix_weights,
    up_partial,
    down_partial,
    up_master,
    down_master,
    up_first,
    down_first,
    up_second,
    down_second,
    counts,
    owner_key,
):
    planes = lax.axis_size("expert") // LINES
    dp_size = lax.axis_size("dp")
    chips = dp_size // CORES
    group = planes // EXPERTS
    steps, rows_dev, model = tokens.shape
    rows = steps * rows_dev
    slab, width = up_master.shape[1:]
    units, columns = down_master.shape[1:]
    bf16, f32 = jnp.bfloat16, jnp.float32

    copies = (
        3 * chips
        + (dp_size - 1)
        + 3 * (LINES - 1)
        + 3 * (chips - 1)
        + (4 + 2 + 2) * (planes - 1)
        + 1
        + (LINES - 1)
        + 2 * chips - 1
        + 2 * (LINES - 1)
    )
    scratch = [
        pltpu.VMEM((rows, model), bf16),
        pltpu.VMEM(up_partial.shape[2:], bf16),
        pltpu.VMEM(down_partial.shape[2:], bf16),
    ]
    for _ in range(4):
        scratch += [pltpu.VMEM((slab, width), f32), pltpu.VMEM((units, columns), f32)]
    scratch += [
        pltpu.VMEM((rows, columns), bf16),
        pltpu.VMEM((group * LINES, rows, slab), bf16),
        pltpu.VMEM((LINES, group, rows, slab), bf16),
        pltpu.VMEM((LINES, group, rows, slab), bf16),
        pltpu.VMEM((8, 128), f32),
        pltpu.VMEM((LINES, 8, 128), f32),
        pltpu.VMEM((8, 128), jnp.int32),
        pltpu.VMEM((dp_size, 8, 128), jnp.int32),
        pltpu.VMEM((chips, slab, width), bf16),
        pltpu.VMEM((chips, units, columns), bf16),
        pltpu.VMEM((chips, slab, width), bf16),
        pltpu.VMEM((chips, units, columns), bf16),
        pltpu.VMEM((chips, slab, width), bf16),
        pltpu.VMEM((chips, units, columns), bf16),
        pltpu.VMEM((planes, slab, width), bf16),
        pltpu.VMEM((planes, units, columns), bf16),
        pltpu.VMEM((EXPERTS, LINES * rows, width), f32),
        pltpu.VMEM((EXPERTS, LINES * rows // 2, width), bf16),
        pltpu.VMEM((EXPERTS, LINES * rows // 2, width), bf16),
        pltpu.VMEM((LINES, EXPERTS, rows, 2 * units), f32),
        pltpu.VMEM((LINES, EXPERTS, rows, 2 * units), bf16),
        pltpu.VMEM((LINES, EXPERTS, rows, 2 * units), bf16),
        pltpu.VMEM((dp_size, EXPERTS, rows, 2 * units), bf16),
        pltpu.VMEM((LINES * rows, planes * units), bf16),
        pltpu.VMEM((LINES, rows, columns), f32),
        pltpu.VMEM((LINES, rows, columns), bf16),
        pltpu.VMEM((LINES, rows, columns), bf16),
        pltpu.SemaphoreType.DMA((copies,)),
        pltpu.SemaphoreType.DMA((copies,)),
        pltpu.SemaphoreType.DMA((12,)),
    ]
    vmem = pl.BlockSpec(memory_space=pltpu.VMEM)
    hbm = pl.BlockSpec(memory_space=pltpu.HBM)
    sizes = (planes, LINES, chips, group, rows, slab, width, units, columns)
    up_update, down_update, decoded = pl.pallas_call(
        functools.partial(kernel, sizes),
        out_shape=(
            jax.ShapeDtypeStruct((slab, width), f32),
            jax.ShapeDtypeStruct((units, columns), f32),
            jax.ShapeDtypeStruct((rows, columns), bf16),
        ),
        in_specs=[pl.BlockSpec(memory_space=pltpu.SMEM), vmem, vmem, vmem] + [hbm] * 9,
        out_specs=(hbm, hbm, hbm),
        scratch_shapes=scratch,
        compiler_params=pltpu.CompilerParams(
            collective_id=0, has_side_effects=True, vmem_limit_bytes=64 * 1024 * 1024
        ),
        cost_estimate=pl.CostEstimate(
            flops=2 * 2 * LINES * rows * planes * slab * width,
            bytes_accessed=6 * 1024 * 1024,
            transcendentals=0,
        ),
    )(
        owner_key,
        routes.transpose(0, 2, 1),
        mix_weights.transpose(0, 2, 1),
        counts,
        tokens.reshape(rows, model),
        up_partial[0, 0],
        down_partial[0, 0],
        up_master[0],
        down_master[0],
        up_first[0],
        down_first[0],
        up_second[0],
        down_second[0],
    )
    results = (up_update, down_update, decoded)
    up_update, down_update, decoded = pl.pallas_call(
        hand_out,
        out_shape=tuple(jax.ShapeDtypeStruct(r.shape, r.dtype) for r in results),
        in_specs=[hbm] * 3,
        out_specs=(hbm,) * 3,
        scratch_shapes=[pltpu.VMEM(r.shape, r.dtype) for r in results]
        + [pltpu.SemaphoreType.DMA((6,))],
        compiler_params=pltpu.CompilerParams(vmem_limit_bytes=64 * 1024 * 1024),
    )(*results)
    return (up_update[None], down_update[None], decoded.reshape(steps, rows_dev, columns))


def solution(mesh):
    return jax.shard_map(
        per_device,
        mesh=mesh,
        in_specs=(
            P(None, "expert", None),
            P(None, "expert", None),
            P(None, "expert", None),
            P("dp", "expert", None, None),
            P("dp", "expert", None, None),
            P("expert", None, "dp"),
            P("expert", None, "dp"),
            P("expert", None, "dp"),
            P("expert", None, "dp"),
            P("expert", None, "dp"),
            P("expert", None, "dp"),
            P("dp", None),
            P(),
        ),
        out_specs=(P("expert", None, "dp"), P("expert", None, "dp"), P(None, "expert", "dp")),
        check_vma=False,
    )
```

```python
import functools

import jax
import jax.numpy as jnp
from jax import lax
from jax.experimental import pallas as pl
from jax.experimental.pallas import tpu as pltpu
from jax.sharding import PartitionSpec as P

EXPERTS = 4
LINES = 4
CORES = 2

beta_one = 0.9
beta_two = 0.95
first_fix = 1.0 - 0.9**10
second_fix = 1.0 - 0.95**10
epsilon = 1e-08
weight_decay = 0.1
learn_rate = 0.001


def adamw_step(gradient, weight, first, second):
    first_new = beta_one * first + (1.0 - beta_one) * gradient
    second_new = beta_two * second + (1.0 - beta_two) * gradient * gradient
    update = (
        first_new / first_fix / (jnp.sqrt(second_new / second_fix) + epsilon)
        + weight_decay * weight
    )
    return (update, weight - learn_rate * update)


class Copy:
    def __init__(self, copy):
        self.copy, self.started, self.landed = copy, False, False

    def start(self):
        self.copy.start()
        self.started = True

    def wait_recv(self):
        self.copy.wait_recv()
        self.landed = True


class Copies:
    def __init__(self, send, recv):
        self.send, self.recv, self.made = send, recv, []

    def make(self, src, dst, device):
        at = len(self.made)
        copy = Copy(
            pltpu.make_async_remote_copy(
                src_ref=src,
                dst_ref=dst,
                send_sem=self.send.at[at],
                recv_sem=self.recv.at[at],
                device_id=device,
                device_id_type=pl.DeviceIdType.MESH,
            )
        )
        self.made.append(copy)
        return copy

    def drain(self):
        for copy in self.made:
            if copy.started:
                copy.copy.wait_send()
                if not copy.landed:
                    copy.copy.wait_recv()


def kernel(
    sizes,
    key_ref,
    routes,
    mix_weights,
    own_counts,
    tokens_far,
    up_partial,
    down_partial,
    up_master_far,
    down_master_far,
    up_first_far,
    down_first_far,
    up_second_far,
    down_second_far,
    up_update_far,
    down_update_far,
    own_far,
    back_far,
    tokens,
    up_own,
    down_own,
    up_master,
    down_master,
    up_first,
    down_first,
    up_second,
    down_second,
    up_update,
    down_update,
    slabs,
    tok_out,
    tok_in,
    gates,
    gates_in,
    counts,
    counts_in,
    up_pair,
    down_pair,
    up_out,
    down_out,
    up_in,
    down_in,
    up_all,
    down_all,
    partial_units,
    swap_out,
    swap_in,
    unit_blocks,
    units_out,
    units_in,
    units_all,
    units_flat,
    back_sum,
    back_out,
    send_sems,
    recv_sems,
    local_sems,
):
    planes, lines, chips, group, rows, slab, width, units, columns = sizes
    dp_size = chips * CORES
    place = lax.axis_index("expert")
    z, y = place // lines, place % lines
    dp = lax.axis_index("dp")
    x, core = dp // CORES, dp % CORES
    key = key_ref[0]
    key_line = key % lines
    key_plane = key // lines % group
    key_group = key // (lines * group)

    def at_plane(step):
        return ((z + step + planes) % planes * lines + y, dp)

    def at_line(step):
        return (z * lines + (y + step) % lines, dp)

    def at_dp(other):
        return (place, other)

    twin = dp + 1 - 2 * core
    lane = lax.broadcasted_iota(jnp.int32, (rows, 2 * units), 1)
    low = lane < units

    def turn(value):
        return pltpu.roll(value, units, value.ndim - 1)

    partners = (
        [at_plane(1), at_plane(-1)]
        + [at_line(k) for k in range(1, lines)]
        + [at_dp((dp + k) % dp_size) for k in range(1, dp_size)]
    )
    barrier = pltpu.get_barrier_semaphore()
    for partner in partners:
        pl.semaphore_signal(
            barrier, inc=1, device_id=partner, device_id_type=pl.DeviceIdType.MESH
        )

    def local(src, dst, at):
        copy = pltpu.make_async_copy(src, dst, local_sems.at[at])
        copy.start()
        return copy

    up_load = local(up_partial, up_own, 0)
    pl.semaphore_wait(barrier, len(partners))

    copies = Copies(send_sems, recv_sems)

    parts = 4
    quarter = slab // parts
    bands = [pl.ds(part * quarter, quarter) for part in range(parts)]
    up_swap, down_swap = [[] for _ in bands], []
    for part in range(parts):
        for chip in range(chips):
            column = pl.multiple_of((chip * CORES + 1 - core) * width, width)
            copy = copies.make(
                up_partial.at[bands[part], pl.ds(column, width)],
                up_pair.at[chip, bands[part]],
                at_dp(twin),
            )
            copy.start()
            up_swap[part].append(copy)

    up_moves, down_moves = [[] for _ in bands], []

    def up_sum(chip, part):
        column = pl.multiple_of((chip * CORES + core) * width, width)
        return up_own[bands[part], pl.ds(column, width)].astype(jnp.float32) + up_pair[
            chip, bands[part]
        ].astype(jnp.float32)

    def down_sum(chip):
        column = pl.multiple_of((chip * CORES + core) * columns, columns)
        return down_own[:, pl.ds(column, columns)].astype(jnp.float32) + down_pair[chip].astype(
            jnp.float32
        )

    def up_send(part):
        for copy in up_swap[part]:
            copy.wait_recv()
        for k in range(1, chips):
            up_out[k, bands[part]] = up_sum((x + k) % chips, part).astype(jnp.bfloat16)
        for k in range(1, chips):
            copy = copies.make(
                up_out.at[k, bands[part]],
                up_in.at[k, bands[part]],
                at_dp((x + k) % chips * CORES + core),
            )
            copy.start()
            up_moves[part].append(copy)

    up_load.wait()
    up_send(0)

    tokens_load = local(tokens_far, tokens, 1)
    up_loads = [
        local(up_master_far, up_master, 2),
        local(up_first_far, up_first, 3),
        local(up_second_far, up_second, 4),
    ]
    up_send(1)
    counts[...] = jnp.zeros_like(counts)
    counts[0:1, 0:EXPERTS] = own_counts[...]
    counts_moves = []
    for k in range(1, dp_size):
        copy = copies.make(counts, counts_in.at[k], at_dp((dp + k) % dp_size))
        copy.start()
        counts_moves.append(copy)
    up_send(2)
    for chip in range(chips):
        column = pl.multiple_of((chip * CORES + 1 - core) * columns, columns)
        copy = copies.make(
            down_partial.at[:, pl.ds(column, columns)], down_pair.at[chip], at_dp(twin)
        )
        copy.start()
        down_swap.append(copy)
    down_loads = [
        local(down_partial, down_own, 5),
        local(down_master_far, down_master, 6),
        local(down_first_far, down_first, 7),
        local(down_second_far, down_second, 8),
    ]
    base = 9
    up_send(3)

    gates[...] = jnp.zeros_like(gates)
    for g in range(EXPERTS):
        chosen = routes[...] == jnp.bitwise_xor(g, key_group)
        gate = jnp.sum(jnp.where(chosen, mix_weights[...], 0.0), axis=1)
        for step in range(gate.shape[0]):
            extent = gate.shape[1]
            gates[g : g + 1, step * extent : (step + 1) * extent] = gate[step : step + 1]

    tokens_load.wait()
    for s in range(group * lines):
        slabs[s] = tokens[:, s * slab : (s + 1) * slab]
    for line in range(lines):
        for plane in range(group):
            which = jnp.bitwise_xor(plane, key_plane) * lines + jnp.bitwise_xor(line, key_line)
            tok_out[line, plane] = slabs[which]
    share = pl.ds(pl.multiple_of(core * (rows // 2), rows // 2), rows // 2)
    token_moves, gate_moves = [], []
    for k in range(1, lines):
        copy = copies.make(tok_out.at[(y + k) % lines, :, share], tok_in.at[y, :, share], at_line(k))
        copy.start()
        token_moves.append(copy)
        copy = copies.make(gates, gates_in.at[y], at_line(k))
        copy.start()
        gate_moves.append(copy)
    tok_in[y] = tok_out[y]
    gates_in[y] = gates[...]

    farthest = planes // 2

    def ring(blocks, parts):
        steps = []
        for step in range(1, farthest + 1):
            made = {}
            for at, (row, column, last_way) in enumerate(parts):
                for way in (1, -1):
                    if step == farthest and way != last_way:
                        continue
                    block = (z - way * (step - 1) + planes) % planes
                    ref = blocks.at[block, row, column]
                    made[at, way] = copies.make(ref, ref, at_plane(way))
            steps.append(made)
        return steps

    def send(steps, parts):
        for (at, _), copy in steps[0].items():
            if at in parts:
                copy.start()

    def pass_on(steps, step):
        onward = steps[step] if step < farthest else {}
        for place_of, copy in steps[step - 1].items():
            copy.wait_recv()
            if place_of in onward:
                onward[place_of].start()

    whole = pl.ds(0, width)
    up_ring = ring(up_all, [(band, whole, 1 - 2 * (at % 2)) for at, band in enumerate(bands)])
    left = columns - columns // 256 * 128
    sides = [(0, left), (left, columns - left)]
    down_rings = [
        ring(
            down_all,
            [
                (pl.ds(at * (units // 2), units // 2), pl.ds(low_column, extent), 1 - 2 * at)
                for at in range(2)
            ],
        )
        for low_column, extent in sides
    ]

    for copy in counts_moves:
        copy.wait_recv()
    totals = counts[...].astype(jnp.float32)
    for k in range(1, dp_size):
        totals = totals + counts_in[k].astype(jnp.float32)
    owner = jnp.bitwise_xor(z // group, key_group)
    label = lax.broadcasted_iota(jnp.int32, totals.shape, 1)
    row_count = jnp.sum(jnp.where(label == owner, totals, 0.0))
    for copy in up_loads:
        copy.wait()
    for part, band in enumerate(bands):
        total = up_sum(x, part)
        for copy in up_moves[part]:
            copy.wait_recv()
        for k in range(1, chips):
            total = total + up_in[k, band].astype(jnp.float32)
        update, new = adamw_step(total / row_count, up_master[band], up_first[band], up_second[band])
        up_update[band] = update
        up_all[z, band] = new.astype(jnp.bfloat16)
        send(up_ring, (part,))
        if part == 1:
            for copy in down_loads:
                copy.wait()
            for copy in down_swap:
                copy.wait_recv()
            for k in range(1, chips):
                chip = (x + k) % chips
                down_out[k] = down_sum(chip).astype(jnp.bfloat16)
                copy = copies.make(down_out.at[k], down_in.at[k], at_dp(chip * CORES + core))
                copy.start()
                down_moves.append(copy)
    writes = [local(up_update, up_update_far, base)]

    pass_on(up_ring, 1)
    total = down_sum(x)
    for copy in down_moves:
        copy.wait_recv()
    for k in range(1, chips):
        total = total + down_in[k].astype(jnp.float32)
    update, new = adamw_step(total / row_count, down_master[...], down_first[...], down_second[...])
    down_update[...] = update
    down_all[z] = new.astype(jnp.bfloat16)
    writes.append(local(down_update, down_update_far, base + 1))
    partial_units[...] = jnp.zeros_like(partial_units)
    pass_on(up_ring, 2)
    twin_moves = []
    for k in range(1, lines):
        token_moves[k - 1].wait_recv()
        gate_moves[k - 1].wait_recv()
        held = tok_in.at[(y - k + lines) % lines, :, share]
        copy = copies.make(held, held, at_dp(twin))
        copy.start()
        twin_moves.append(copy)

    def meet(block):
        held = tok_in[:, block % group].reshape(lines * rows, slab)
        product = jnp.dot(held, up_all[block], preferred_element_type=jnp.float32)
        partial_units[block // group] = partial_units[block // group] + product

    def meet_step(step):
        meet((z - step + planes) % planes)
        if step < farthest:
            meet((z + step) % planes)

    def down_pass(first, second):
        if first:
            pass_on(down_rings[0], first)
        if second:
            pass_on(down_rings[1], second)

    half = lines * rows // 2
    mine = pl.ds(pl.multiple_of(core * half, half), half)
    other = pl.ds(pl.multiple_of((1 - core) * half, half), half)
    order = (0, 1, 3, 2)

    def holder(at):
        return (z // group + order[at]) % EXPERTS

    class Units:
        def __init__(self, first, count):
            self.ats, self.span = range(first, first + count), pl.ds(first, count)

        def swap(self):
            for at in self.ats:
                swap_out[at] = partial_units[holder(at), other].astype(jnp.bfloat16)
            self.swapped = copies.make(
                swap_out.at[self.span], swap_in.at[self.span], at_dp(twin)
            )
            self.swapped.start()

        def along_lines(self):
            def blocks_of(value, at, first):
                upper, lower = value[:rows], value[rows:]
                unit_blocks[first, at] = jnp.where(low, upper, turn(lower))
                unit_blocks[first + 1, at] = jnp.where(low, turn(upper), lower)

            for at in self.ats:
                blocks_of(partial_units[holder(at), mine], at, 2 * core)
            self.swapped.wait_recv()
            for at in self.ats:
                blocks_of(swap_in[at].astype(jnp.float32), at, 2 * (1 - core))
            self.moves = []
            for k in range(1, lines):
                block = jnp.bitwise_xor((y + k) % lines, key_line)
                for at in self.ats:
                    units_out[k, at] = unit_blocks[block, at].astype(jnp.bfloat16)
                copy = copies.make(
                    units_out.at[k, self.span], units_in.at[k, self.span], at_line(k)
                )
                copy.start()
                self.moves.append(copy)

        def over_dp(self):
            for copy in self.moves:
                copy.wait_recv()
            upper, lower = gates_in[2 * core].T[:rows], gates_in[2 * core + 1].T[:rows]
            label = lax.broadcasted_iota(jnp.int32, upper.shape, 1)
            for at in self.ats:
                summed = unit_blocks[jnp.bitwise_xor(y, key_line), at]
                for k in range(1, lines):
                    summed = summed + units_in[k, at].astype(jnp.float32)
                gate = [
                    jnp.sum(jnp.where(label == holder(at), value, 0.0), axis=1, keepdims=True)
                    for value in (upper, lower)
                ]
                gated = jax.nn.silu(summed) * jnp.where(low, gate[0], gate[1])
                units_all[dp, at] = gated.astype(jnp.bfloat16)
            self.moves = []
            held = units_all.at[dp, self.span]
            for k in range(1, chips):
                copy = copies.make(held, held, at_dp((x + k) % chips * CORES + core))
                copy.start()
                self.moves.append(copy)
            self.twin_moves = [copies.make(held, held, at_dp(twin))]
            self.twin_moves[0].start()

        def to_twin(self):
            for k in range(1, chips):
                self.moves[k - 1].wait_recv()
                held = units_all.at[(x - k + chips) % chips * CORES + core, self.span]
                copy = copies.make(held, held, at_dp(twin))
                copy.start()
                self.twin_moves.append(copy)

        def landed(self):
            for copy in self.twin_moves:
                copy.wait_recv()

        def flat(self):
            for at in self.ats:
                for pair in range(group // 2):
                    column = (at * group + 2 * pair) * units
                    for owner_core in range(CORES):
                        even, odd = (
                            units_all[
                                jnp.bitwise_xor(2 * pair + n, key_plane) * CORES + owner_core, at
                            ].astype(jnp.float32)
                            for n in range(2)
                        )
                        row = owner_core * half
                        units_flat[row : row + rows, column : column + 2 * units] = jnp.where(
                            low, even, turn(odd)
                        ).astype(jnp.bfloat16)
                        units_flat[row + rows : row + half, column : column + 2 * units] = (
                            jnp.where(low, turn(even), odd).astype(jnp.bfloat16)
                        )

    near, far = Units(0, EXPERTS - 1), Units(EXPERTS - 1, 1)
    lag_left, lag_right = 2, 3

    def down_pass(step):
        for blocks, lag in ((down_rings[0], lag_left), (down_rings[1], lag_right)):
            if 1 <= step - lag <= farthest:
                pass_on(blocks, step - lag)
            if step == lag:
                send(blocks, (0, 1))

    down_pass(2)
    pass_on(up_ring, 3)
    down_pass(3)
    for copy in twin_moves:
        copy.wait_recv()
    meet(z)
    meet_step(1)
    pass_on(up_ring, 4)
    down_pass(4)
    meet_step(2)
    meet_step(3)
    for step in range(5, farthest):
        pass_on(up_ring, step)
        down_pass(step)
        meet_step(step - 1)
    meet_step(farthest - 1)
    near.swap()
    near.along_lines()
    pass_on(up_ring, farthest)
    meet_step(farthest)
    far.swap()
    far.along_lines()
    near.over_dp()
    down_pass(farthest)
    far.over_dp()
    down_pass(farthest + 1)
    near.to_twin()
    far.to_twin()
    for step in range(farthest + 2, farthest + lag_left + 1):
        down_pass(step)
    near.landed()
    far.landed()
    near.flat()
    far.flat()

    back_moves = []
    for side, (low_column, extent) in enumerate(sides):
        if side == 1:
            for step in range(farthest + lag_left + 1, farthest + lag_right + 1):
                down_pass(step)
        side_columns = pl.ds(low_column, extent)
        product = jnp.zeros((lines * rows, extent), jnp.float32)
        for at in range(EXPERTS):
            held = down_all[pl.ds(holder(at) * group, group), :, side_columns]
            product = product + jnp.dot(
                units_flat[:, at * group * units : (at + 1) * group * units],
                held.reshape(group * units, extent),
                preferred_element_type=jnp.float32,
            )
        product = product.reshape(lines, rows, extent)
        back_sum[:, :, side_columns] = product
        back_out[:, :, side_columns] = product.astype(jnp.bfloat16)
        for k in range(1, lines):
            copy = copies.make(
                back_out.at[(y + k) % lines, :, side_columns],
                back_far.at[k - 1, :, side_columns],
                at_line(k),
            )
            copy.start()
            back_moves.append(copy)
    writes.append(local(back_sum.at[y], own_far, base + 2))
    for copy in back_moves:
        copy.wait_recv()
    for copy in writes:
        copy.wait()

    copies.drain()


def hand_out(a, b, own, back, a_out, b_out, out, a_held, b_held, own_held, back_held, held, sems):
    reads = [
        pltpu.make_async_copy(src, dst, sems.at[at])
        for at, (src, dst) in enumerate(
            ((own, own_held), (back, back_held), (a, a_held), (b, b_held))
        )
    ]
    writes = [
        pltpu.make_async_copy(src, dst, sems.at[4 + at])
        for at, (src, dst) in enumerate(((held, out), (a_held, a_out), (b_held, b_out)))
    ]
    for copy in reads:
        copy.start()
    reads[0].wait()
    reads[1].wait()
    result = own_held[...]
    for k in range(back_held.shape[0]):
        result = result + back_held[k].astype(jnp.float32)
    held[...] = result.astype(held.dtype)
    writes[0].start()
    reads[2].wait()
    writes[1].start()
    reads[3].wait()
    writes[2].start()
    for copy in writes:
        copy.wait()


def per_device(
    tokens,
    routes,
    mix_weights,
    up_partial,
    down_partial,
    up_master,
    down_master,
    up_first,
    down_first,
    up_second,
    down_second,
    counts,
    owner_key,
):
    planes = lax.axis_size("expert") // LINES
    dp_size = lax.axis_size("dp")
    chips = dp_size // CORES
    group = planes // EXPERTS
    steps, rows_dev, model = tokens.shape
    rows = steps * rows_dev
    slab, width = up_master.shape[1:]
    units, columns = down_master.shape[1:]
    bf16, f32 = jnp.bfloat16, jnp.float32

    copies = (
        (4 + 1) * chips
        + (dp_size - 1)
        + 3 * (LINES - 1)
        + (4 + 1) * (chips - 1)
        + (4 + 2 + 2) * (planes - 1)
        + 2 * 1
        + 2 * (LINES - 1)
        + 2 * (2 * chips - 1)
        + 2 * (LINES - 1)
    )
    scratch = [
        pltpu.VMEM((rows, model), bf16),
        pltpu.VMEM(up_partial.shape[2:], bf16),
        pltpu.VMEM(down_partial.shape[2:], bf16),
    ]
    for _ in range(4):
        scratch += [pltpu.VMEM((slab, width), f32), pltpu.VMEM((units, columns), f32)]
    scratch += [
        pltpu.VMEM((group * LINES, rows, slab), bf16),
        pltpu.VMEM((LINES, group, rows, slab), bf16),
        pltpu.VMEM((LINES, group, rows, slab), bf16),
        pltpu.VMEM((8, 128), f32),
        pltpu.VMEM((LINES, 8, 128), f32),
        pltpu.VMEM((8, 128), jnp.int32),
        pltpu.VMEM((dp_size, 8, 128), jnp.int32),
        pltpu.VMEM((chips, slab, width), bf16),
        pltpu.VMEM((chips, units, columns), bf16),
        pltpu.VMEM((chips, slab, width), bf16),
        pltpu.VMEM((chips, units, columns), bf16),
        pltpu.VMEM((chips, slab, width), bf16),
        pltpu.VMEM((chips, units, columns), bf16),
        pltpu.VMEM((planes, slab, width), bf16),
        pltpu.VMEM((planes, units, columns), bf16),
        pltpu.VMEM((EXPERTS, LINES * rows, width), f32),
        pltpu.VMEM((EXPERTS, LINES * rows // 2, width), bf16),
        pltpu.VMEM((EXPERTS, LINES * rows // 2, width), bf16),
        pltpu.VMEM((LINES, EXPERTS, rows, 2 * units), f32),
        pltpu.VMEM((LINES, EXPERTS, rows, 2 * units), bf16),
        pltpu.VMEM((LINES, EXPERTS, rows, 2 * units), bf16),
        pltpu.VMEM((dp_size, EXPERTS, rows, 2 * units), bf16),
        pltpu.VMEM((LINES * rows, planes * units), bf16),
        pltpu.VMEM((LINES, rows, columns), f32),
        pltpu.VMEM((LINES, rows, columns), bf16),
        pltpu.SemaphoreType.DMA((copies,)),
        pltpu.SemaphoreType.DMA((copies,)),
        pltpu.SemaphoreType.DMA((12,)),
    ]
    vmem = pl.BlockSpec(memory_space=pltpu.VMEM)
    hbm = pl.BlockSpec(memory_space=pltpu.HBM)
    sizes = (planes, LINES, chips, group, rows, slab, width, units, columns)
    results = pl.pallas_call(
        functools.partial(kernel, sizes),
        out_shape=(
            jax.ShapeDtypeStruct((slab, width), f32),
            jax.ShapeDtypeStruct((units, columns), f32),
            jax.ShapeDtypeStruct((rows, columns), f32),
            jax.ShapeDtypeStruct((LINES - 1, rows, columns), bf16),
        ),
        in_specs=[pl.BlockSpec(memory_space=pltpu.SMEM), vmem, vmem, vmem] + [hbm] * 9,
        out_specs=(hbm,) * 4,
        scratch_shapes=scratch,
        compiler_params=pltpu.CompilerParams(
            collective_id=0, has_side_effects=True, vmem_limit_bytes=64 * 1024 * 1024
        ),
        cost_estimate=pl.CostEstimate(
            flops=2 * 2 * LINES * rows * planes * slab * width,
            bytes_accessed=6 * 1024 * 1024,
            transcendentals=0,
        ),
    )(
        owner_key,
        routes.transpose(0, 2, 1),
        mix_weights.transpose(0, 2, 1),
        counts,
        tokens.reshape(rows, model),
        up_partial[0, 0],
        down_partial[0, 0],
        up_master[0],
        down_master[0],
        up_first[0],
        down_first[0],
        up_second[0],
        down_second[0],
    )
    out_shapes = [((slab, width), f32), ((units, columns), f32), ((rows, columns), bf16)]
    up_update, down_update, decoded = pl.pallas_call(
        hand_out,
        out_shape=tuple(jax.ShapeDtypeStruct(*shape) for shape in out_shapes),
        in_specs=[hbm] * 4,
        out_specs=(hbm,) * 3,
        scratch_shapes=[pltpu.VMEM(r.shape, r.dtype) for r in results]
        + [pltpu.VMEM((rows, columns), bf16), pltpu.SemaphoreType.DMA((7,))],
        compiler_params=pltpu.CompilerParams(vmem_limit_bytes=64 * 1024 * 1024),
    )(*results)
    return (up_update[None], down_update[None], decoded.reshape(steps, rows_dev, columns))


def solution(mesh):
    return jax.shard_map(
        per_device,
        mesh=mesh,
        in_specs=(
            P(None, "expert", None),
            P(None, "expert", None),
            P(None, "expert", None),
            P("dp", "expert", None, None),
            P("dp", "expert", None, None),
            P("expert", None, "dp"),
            P("expert", None, "dp"),
            P("expert", None, "dp"),
            P("expert", None, "dp"),
            P("expert", None, "dp"),
            P("expert", None, "dp"),
            P("dp", None),
            P(),
        ),
        out_specs=(P("expert", None, "dp"), P("expert", None, "dp"), P(None, "expert", "dp")),
        check_vma=False,
    )
```

```python
import functools

import jax
import jax.numpy as jnp
from jax import lax
from jax.experimental import pallas as pl
from jax.experimental.pallas import tpu as pltpu
from jax.sharding import PartitionSpec as P

EXPERTS = 4
LINES = 4
CORES = 2

beta_one = 0.9
beta_two = 0.95
first_fix = 1.0 - 0.9**10
second_fix = 1.0 - 0.95**10
epsilon = 1e-08
weight_decay = 0.1
learn_rate = 0.001


def adamw_step(gradient, weight, first, second):
    first_new = beta_one * first + (1.0 - beta_one) * gradient
    second_new = beta_two * second + (1.0 - beta_two) * gradient * gradient
    update = (
        first_new / first_fix / (jnp.sqrt(second_new / second_fix) + epsilon)
        + weight_decay * weight
    )
    return (update, weight - learn_rate * update)


class Copy:
    def __init__(self, copy):
        self.copy, self.started, self.landed = copy, False, False

    def start(self):
        self.copy.start()
        self.started = True

    def wait_recv(self):
        self.copy.wait_recv()
        self.landed = True


class Copies:
    def __init__(self, send, recv):
        self.send, self.recv, self.made = send, recv, []

    def make(self, src, dst, device):
        at = len(self.made)
        copy = Copy(
            pltpu.make_async_remote_copy(
                src_ref=src,
                dst_ref=dst,
                send_sem=self.send.at[at],
                recv_sem=self.recv.at[at],
                device_id=device,
                device_id_type=pl.DeviceIdType.MESH,
            )
        )
        self.made.append(copy)
        return copy

    def drain(self):
        for copy in self.made:
            if copy.started:
                copy.copy.wait_send()
                if not copy.landed:
                    copy.copy.wait_recv()


def kernel(
    sizes,
    key_ref,
    routes,
    mix_weights,
    own_counts,
    tokens_far,
    up_partial,
    down_partial,
    up_master_far,
    down_master_far,
    up_first_far,
    down_first_far,
    up_second_far,
    down_second_far,
    up_update_far,
    down_update_far,
    own_far,
    back_far,
    tokens,
    up_own,
    down_own,
    up_master,
    down_master,
    up_first,
    down_first,
    up_second,
    down_second,
    up_update,
    down_update,
    slabs,
    tok_out,
    tok_in,
    gates,
    gates_in,
    counts,
    counts_in,
    up_pair,
    down_pair,
    up_out,
    down_out,
    up_in,
    down_in,
    up_all,
    down_all,
    partial_units,
    swap_out,
    swap_in,
    unit_blocks,
    units_out,
    units_in,
    units_all,
    units_flat,
    back_sum,
    back_out,
    send_sems,
    recv_sems,
    local_sems,
):
    planes, lines, chips, group, rows, slab, width, units, columns = sizes
    dp_size = chips * CORES
    place = lax.axis_index("expert")
    z, y = place // lines, place % lines
    dp = lax.axis_index("dp")
    x, core = dp // CORES, dp % CORES
    key = key_ref[0]
    key_line = key % lines
    key_plane = key // lines % group
    key_group = key // (lines * group)

    def at_plane(step):
        return ((z + step + planes) % planes * lines + y, dp)

    def at_line(step):
        return (z * lines + (y + step) % lines, dp)

    def at_dp(other):
        return (place, other)

    twin = dp + 1 - 2 * core
    lane = lax.broadcasted_iota(jnp.int32, (rows, 2 * units), 1)
    low = lane < units

    def turn(value):
        return pltpu.roll(value, units, value.ndim - 1)

    partners = (
        [at_plane(1), at_plane(-1)]
        + [at_line(k) for k in range(1, lines)]
        + [at_dp((dp + k) % dp_size) for k in range(1, dp_size)]
    )
    barrier = pltpu.get_barrier_semaphore()
    for partner in partners:
        pl.semaphore_signal(
            barrier, inc=1, device_id=partner, device_id_type=pl.DeviceIdType.MESH
        )

    def local(src, dst, at):
        copy = pltpu.make_async_copy(src, dst, local_sems.at[at])
        copy.start()
        return copy

    up_load = local(up_partial, up_own, 0)
    pl.semaphore_wait(barrier, len(partners))

    copies = Copies(send_sems, recv_sems)

    parts = 4
    quarter = slab // parts
    bands = [pl.ds(part * quarter, quarter) for part in range(parts)]
    up_swap, down_swap = [[] for _ in bands], []
    for part in range(parts):
        for chip in range(chips):
            column = pl.multiple_of((chip * CORES + 1 - core) * width, width)
            copy = copies.make(
                up_partial.at[bands[part], pl.ds(column, width)],
                up_pair.at[chip, bands[part]],
                at_dp(twin),
            )
            copy.start()
            up_swap[part].append(copy)

    up_moves, down_moves = [[] for _ in bands], []

    def up_sum(chip, part):
        column = pl.multiple_of((chip * CORES + core) * width, width)
        return up_own[bands[part], pl.ds(column, width)].astype(jnp.float32) + up_pair[
            chip, bands[part]
        ].astype(jnp.float32)

    def down_sum(chip):
        column = pl.multiple_of((chip * CORES + core) * columns, columns)
        return down_own[:, pl.ds(column, columns)].astype(jnp.float32) + down_pair[chip].astype(
            jnp.float32
        )

    def up_send(part):
        for copy in up_swap[part]:
            copy.wait_recv()
        for k in range(1, chips):
            up_out[k, bands[part]] = up_sum((x + k) % chips, part).astype(jnp.bfloat16)
        for k in range(1, chips):
            copy = copies.make(
                up_out.at[k, bands[part]],
                up_in.at[k, bands[part]],
                at_dp((x + k) % chips * CORES + core),
            )
            copy.start()
            up_moves[part].append(copy)

    up_load.wait()
    up_send(0)

    tokens_load = local(tokens_far, tokens, 1)
    up_loads = [
        local(up_master_far, up_master, 2),
        local(up_first_far, up_first, 3),
        local(up_second_far, up_second, 4),
    ]
    up_send(1)
    counts[...] = jnp.zeros_like(counts)
    counts[0:1, 0:EXPERTS] = own_counts[...]
    counts_moves = []
    for k in range(1, dp_size):
        copy = copies.make(counts, counts_in.at[k], at_dp((dp + k) % dp_size))
        copy.start()
        counts_moves.append(copy)
    up_send(2)
    for chip in range(chips):
        column = pl.multiple_of((chip * CORES + 1 - core) * columns, columns)
        copy = copies.make(
            down_partial.at[:, pl.ds(column, columns)], down_pair.at[chip], at_dp(twin)
        )
        copy.start()
        down_swap.append(copy)
    down_loads = [
        local(down_partial, down_own, 5),
        local(down_master_far, down_master, 6),
        local(down_first_far, down_first, 7),
        local(down_second_far, down_second, 8),
    ]
    base = 9
    up_send(3)

    gates[...] = jnp.zeros_like(gates)
    for g in range(EXPERTS):
        chosen = routes[...] == jnp.bitwise_xor(g, key_group)
        gate = jnp.sum(jnp.where(chosen, mix_weights[...], 0.0), axis=1)
        for step in range(gate.shape[0]):
            extent = gate.shape[1]
            gates[g : g + 1, step * extent : (step + 1) * extent] = gate[step : step + 1]

    tokens_load.wait()
    for s in range(group * lines):
        slabs[s] = tokens[:, s * slab : (s + 1) * slab]
    for line in range(lines):
        for plane in range(group):
            which = jnp.bitwise_xor(plane, key_plane) * lines + jnp.bitwise_xor(line, key_line)
            tok_out[line, plane] = slabs[which]
    share = pl.ds(pl.multiple_of(core * (rows // 2), rows // 2), rows // 2)
    token_moves, gate_moves = [], []
    for k in range(1, lines):
        copy = copies.make(tok_out.at[(y + k) % lines, :, share], tok_in.at[y, :, share], at_line(k))
        copy.start()
        token_moves.append(copy)
        copy = copies.make(gates, gates_in.at[y], at_line(k))
        copy.start()
        gate_moves.append(copy)
    tok_in[y] = tok_out[y]
    gates_in[y] = gates[...]

    farthest = planes // 2

    def ring(blocks, parts):
        steps = []
        for step in range(1, farthest + 1):
            made = {}
            for at, (row, column, last_way) in enumerate(parts):
                for way in (1, -1):
                    if step == farthest and way != last_way:
                        continue
                    block = (z - way * (step - 1) + planes) % planes
                    ref = blocks.at[block, row, column]
                    made[at, way] = copies.make(ref, ref, at_plane(way))
            steps.append(made)
        return steps

    def send(steps, parts):
        for (at, _), copy in steps[0].items():
            if at in parts:
                copy.start()

    def pass_on(steps, step):
        onward = steps[step] if step < farthest else {}
        for place_of, copy in steps[step - 1].items():
            copy.wait_recv()
            if place_of in onward:
                onward[place_of].start()

    whole = pl.ds(0, width)
    up_ring = ring(up_all, [(band, whole, 1 - 2 * (at % 2)) for at, band in enumerate(bands)])
    left = columns - columns // 256 * 128
    sides = [(0, left), (left, columns - left)]
    down_rings = [
        ring(
            down_all,
            [
                (pl.ds(at * (units // 2), units // 2), pl.ds(low_column, extent), 1 - 2 * at)
                for at in range(2)
            ],
        )
        for low_column, extent in sides
    ]

    for copy in counts_moves:
        copy.wait_recv()
    totals = counts[...].astype(jnp.float32)
    for k in range(1, dp_size):
        totals = totals + counts_in[k].astype(jnp.float32)
    owner = jnp.bitwise_xor(z // group, key_group)
    label = lax.broadcasted_iota(jnp.int32, totals.shape, 1)
    row_count = jnp.sum(jnp.where(label == owner, totals, 0.0))
    for copy in up_loads:
        copy.wait()
    for part, band in enumerate(bands):
        total = up_sum(x, part)
        for copy in up_moves[part]:
            copy.wait_recv()
        for k in range(1, chips):
            total = total + up_in[k, band].astype(jnp.float32)
        update, new = adamw_step(total / row_count, up_master[band], up_first[band], up_second[band])
        up_update[band] = update
        up_all[z, band] = new.astype(jnp.bfloat16)
        send(up_ring, (part,))
        if part == 1:
            for copy in down_loads:
                copy.wait()
            for copy in down_swap:
                copy.wait_recv()
            for k in range(1, chips):
                chip = (x + k) % chips
                down_out[k] = down_sum(chip).astype(jnp.bfloat16)
                copy = copies.make(down_out.at[k], down_in.at[k], at_dp(chip * CORES + core))
                copy.start()
                down_moves.append(copy)
    writes = [local(up_update, up_update_far, base)]

    pass_on(up_ring, 1)
    total = down_sum(x)
    for copy in down_moves:
        copy.wait_recv()
    for k in range(1, chips):
        total = total + down_in[k].astype(jnp.float32)
    update, new = adamw_step(total / row_count, down_master[...], down_first[...], down_second[...])
    down_update[...] = update
    down_all[z] = new.astype(jnp.bfloat16)
    writes.append(local(down_update, down_update_far, base + 1))
    partial_units[...] = jnp.zeros_like(partial_units)
    pass_on(up_ring, 2)
    twin_moves = []
    for k in range(1, lines):
        token_moves[k - 1].wait_recv()
        gate_moves[k - 1].wait_recv()
        held = tok_in.at[(y - k + lines) % lines, :, share]
        copy = copies.make(held, held, at_dp(twin))
        copy.start()
        twin_moves.append(copy)

    def meet(block):
        held = tok_in[:, block % group].reshape(lines * rows, slab)
        product = jnp.dot(held, up_all[block], preferred_element_type=jnp.float32)
        partial_units[block // group] = partial_units[block // group] + product

    def meet_step(step):
        meet((z - step + planes) % planes)
        if step < farthest:
            meet((z + step) % planes)

    def down_pass(first, second):
        if first:
            pass_on(down_rings[0], first)
        if second:
            pass_on(down_rings[1], second)

    half = lines * rows // 2
    mine = pl.ds(pl.multiple_of(core * half, half), half)
    other = pl.ds(pl.multiple_of((1 - core) * half, half), half)
    order = (0, 1, 3, 2)

    def holder(at):
        return (z // group + order[at]) % EXPERTS

    class Units:
        def __init__(self, first, count):
            self.ats, self.span = range(first, first + count), pl.ds(first, count)

        def swap(self):
            for at in self.ats:
                swap_out[at] = partial_units[holder(at), other].astype(jnp.bfloat16)
            self.swapped = copies.make(
                swap_out.at[self.span], swap_in.at[self.span], at_dp(twin)
            )
            self.swapped.start()

        def along_lines(self):
            def blocks_of(value, at, first):
                upper, lower = value[:rows], value[rows:]
                unit_blocks[first, at] = jnp.where(low, upper, turn(lower))
                unit_blocks[first + 1, at] = jnp.where(low, turn(upper), lower)

            for at in self.ats:
                blocks_of(partial_units[holder(at), mine], at, 2 * core)
            self.swapped.wait_recv()
            for at in self.ats:
                blocks_of(swap_in[at].astype(jnp.float32), at, 2 * (1 - core))
            self.moves = []
            for k in range(1, lines):
                block = jnp.bitwise_xor((y + k) % lines, key_line)
                for at in self.ats:
                    units_out[k, at] = unit_blocks[block, at].astype(jnp.bfloat16)
                copy = copies.make(
                    units_out.at[k, self.span], units_in.at[k, self.span], at_line(k)
                )
                copy.start()
                self.moves.append(copy)

        def over_dp(self):
            for copy in self.moves:
                copy.wait_recv()
            upper, lower = gates_in[2 * core].T[:rows], gates_in[2 * core + 1].T[:rows]
            label = lax.broadcasted_iota(jnp.int32, upper.shape, 1)
            for at in self.ats:
                summed = unit_blocks[jnp.bitwise_xor(y, key_line), at]
                for k in range(1, lines):
                    summed = summed + units_in[k, at].astype(jnp.float32)
                gate = [
                    jnp.sum(jnp.where(label == holder(at), value, 0.0), axis=1, keepdims=True)
                    for value in (upper, lower)
                ]
                gated = jax.nn.silu(summed) * jnp.where(low, gate[0], gate[1])
                units_all[dp, at] = gated.astype(jnp.bfloat16)
            held = units_all.at[dp, self.span]
            if len(self.ats) == 1:
                targets = [(dp + k) % dp_size for k in range(1, dp_size)]
            else:
                targets = [(x + k) % chips * CORES + core for k in range(1, chips)] + [twin]
            self.moves = []
            for target in targets:
                copy = copies.make(held, held, at_dp(target))
                copy.start()
                self.moves.append(copy)

        def to_twin(self):
            self.twin_moves = self.moves[chips - 1 :]
            for k in range(1, chips):
                self.moves[k - 1].wait_recv()
                held = units_all.at[(x - k + chips) % chips * CORES + core, self.span]
                copy = copies.make(held, held, at_dp(twin))
                copy.start()
                self.twin_moves.append(copy)

        def landed(self):
            for copy in self.moves if len(self.ats) == 1 else self.twin_moves:
                copy.wait_recv()

        def flat(self):
            for at in self.ats:
                for pair in range(group // 2):
                    column = (at * group + 2 * pair) * units
                    for owner_core in range(CORES):
                        even, odd = (
                            units_all[
                                jnp.bitwise_xor(2 * pair + n, key_plane) * CORES + owner_core, at
                            ].astype(jnp.float32)
                            for n in range(2)
                        )
                        row = owner_core * half
                        units_flat[row : row + rows, column : column + 2 * units] = jnp.where(
                            low, even, turn(odd)
                        ).astype(jnp.bfloat16)
                        units_flat[row + rows : row + half, column : column + 2 * units] = (
                            jnp.where(low, turn(even), odd).astype(jnp.bfloat16)
                        )

    near, far = Units(0, EXPERTS - 1), Units(EXPERTS - 1, 1)
    lag_left, lag_right = 3, 3

    def down_pass(step):
        for blocks, lag in ((down_rings[0], lag_left), (down_rings[1], lag_right)):
            if 1 <= step - lag <= farthest:
                pass_on(blocks, step - lag)
            if step == lag:
                send(blocks, (0, 1))

    down_pass(2)
    pass_on(up_ring, 3)
    down_pass(3)
    for copy in twin_moves:
        copy.wait_recv()
    meet(z)
    meet_step(1)
    pass_on(up_ring, 4)
    down_pass(4)
    meet_step(2)
    meet_step(3)
    for step in range(5, farthest):
        pass_on(up_ring, step)
        down_pass(step)
        meet_step(step - 1)
    meet_step(farthest - 1)
    near.swap()
    near.along_lines()
    pass_on(up_ring, farthest)
    meet_step(farthest)
    far.swap()
    down_pass(farthest)
    far.along_lines()
    near.over_dp()
    far.over_dp()
    down_pass(farthest + 1)
    near.to_twin()
    for step in range(farthest + 2, farthest + lag_left + 1):
        down_pass(step)
    near.landed()
    far.landed()
    near.flat()
    far.flat()

    back_moves = []
    for side, (low_column, extent) in enumerate(sides):
        if side == 1:
            for step in range(farthest + lag_left + 1, farthest + lag_right + 1):
                down_pass(step)
        side_columns = pl.ds(low_column, extent)
        product = jnp.zeros((lines * rows, extent), jnp.float32)
        for at in range(EXPERTS):
            held = down_all[pl.ds(holder(at) * group, group), :, side_columns]
            product = product + jnp.dot(
                units_flat[:, at * group * units : (at + 1) * group * units],
                held.reshape(group * units, extent),
                preferred_element_type=jnp.float32,
            )
        product = product.reshape(lines, rows, extent)
        back_sum[:, :, side_columns] = product
        back_out[:, :, side_columns] = product.astype(jnp.bfloat16)
        for k in range(1, lines):
            copy = copies.make(
                back_out.at[(y + k) % lines, :, side_columns],
                back_far.at[k - 1, :, side_columns],
                at_line(k),
            )
            copy.start()
            back_moves.append(copy)
    writes.append(local(back_sum.at[y], own_far, base + 2))
    for copy in back_moves:
        copy.wait_recv()
    for copy in writes:
        copy.wait()

    copies.drain()


def hand_out(a, b, own, back, a_out, b_out, out, a_held, b_held, own_held, back_held, held, sems):
    reads = [
        pltpu.make_async_copy(src, dst, sems.at[at])
        for at, (src, dst) in enumerate(
            ((own, own_held), (back, back_held), (a, a_held), (b, b_held))
        )
    ]
    writes = [
        pltpu.make_async_copy(src, dst, sems.at[4 + at])
        for at, (src, dst) in enumerate(((held, out), (a_held, a_out), (b_held, b_out)))
    ]
    for copy in reads:
        copy.start()
    reads[0].wait()
    reads[1].wait()
    result = own_held[...]
    for k in range(back_held.shape[0]):
        result = result + back_held[k].astype(jnp.float32)
    held[...] = result.astype(held.dtype)
    writes[0].start()
    reads[2].wait()
    writes[1].start()
    reads[3].wait()
    writes[2].start()
    for copy in writes:
        copy.wait()


def per_device(
    tokens,
    routes,
    mix_weights,
    up_partial,
    down_partial,
    up_master,
    down_master,
    up_first,
    down_first,
    up_second,
    down_second,
    counts,
    owner_key,
):
    planes = lax.axis_size("expert") // LINES
    dp_size = lax.axis_size("dp")
    chips = dp_size // CORES
    group = planes // EXPERTS
    steps, rows_dev, model = tokens.shape
    rows = steps * rows_dev
    slab, width = up_master.shape[1:]
    units, columns = down_master.shape[1:]
    bf16, f32 = jnp.bfloat16, jnp.float32

    copies = (
        (4 + 1) * chips
        + (dp_size - 1)
        + 3 * (LINES - 1)
        + (4 + 1) * (chips - 1)
        + (4 + 2 + 2) * (planes - 1)
        + 2 * 1
        + 2 * (LINES - 1)
        + (2 * chips - 1) + (dp_size - 1)
        + 2 * (LINES - 1)
    )
    scratch = [
        pltpu.VMEM((rows, model), bf16),
        pltpu.VMEM(up_partial.shape[2:], bf16),
        pltpu.VMEM(down_partial.shape[2:], bf16),
    ]
    for _ in range(4):
        scratch += [pltpu.VMEM((slab, width), f32), pltpu.VMEM((units, columns), f32)]
    scratch += [
        pltpu.VMEM((group * LINES, rows, slab), bf16),
        pltpu.VMEM((LINES, group, rows, slab), bf16),
        pltpu.VMEM((LINES, group, rows, slab), bf16),
        pltpu.VMEM((8, 128), f32),
        pltpu.VMEM((LINES, 8, 128), f32),
        pltpu.VMEM((8, 128), jnp.int32),
        pltpu.VMEM((dp_size, 8, 128), jnp.int32),
        pltpu.VMEM((chips, slab, width), bf16),
        pltpu.VMEM((chips, units, columns), bf16),
        pltpu.VMEM((chips, slab, width), bf16),
        pltpu.VMEM((chips, units, columns), bf16),
        pltpu.VMEM((chips, slab, width), bf16),
        pltpu.VMEM((chips, units, columns), bf16),
        pltpu.VMEM((planes, slab, width), bf16),
        pltpu.VMEM((planes, units, columns), bf16),
        pltpu.VMEM((EXPERTS, LINES * rows, width), f32),
        pltpu.VMEM((EXPERTS, LINES * rows // 2, width), bf16),
        pltpu.VMEM((EXPERTS, LINES * rows // 2, width), bf16),
        pltpu.VMEM((LINES, EXPERTS, rows, 2 * units), f32),
        pltpu.VMEM((LINES, EXPERTS, rows, 2 * units), bf16),
        pltpu.VMEM((LINES, EXPERTS, rows, 2 * units), bf16),
        pltpu.VMEM((dp_size, EXPERTS, rows, 2 * units), bf16),
        pltpu.VMEM((LINES * rows, planes * units), bf16),
        pltpu.VMEM((LINES, rows, columns), f32),
        pltpu.VMEM((LINES, rows, columns), bf16),
        pltpu.SemaphoreType.DMA((copies,)),
        pltpu.SemaphoreType.DMA((copies,)),
        pltpu.SemaphoreType.DMA((12,)),
    ]
    vmem = pl.BlockSpec(memory_space=pltpu.VMEM)
    hbm = pl.BlockSpec(memory_space=pltpu.HBM)
    sizes = (planes, LINES, chips, group, rows, slab, width, units, columns)
    results = pl.pallas_call(
        functools.partial(kernel, sizes),
        out_shape=(
            jax.ShapeDtypeStruct((slab, width), f32),
            jax.ShapeDtypeStruct((units, columns), f32),
            jax.ShapeDtypeStruct((rows, columns), f32),
            jax.ShapeDtypeStruct((LINES - 1, rows, columns), bf16),
        ),
        in_specs=[pl.BlockSpec(memory_space=pltpu.SMEM), vmem, vmem, vmem] + [hbm] * 9,
        out_specs=(hbm,) * 4,
        scratch_shapes=scratch,
        compiler_params=pltpu.CompilerParams(
            collective_id=0, has_side_effects=True, vmem_limit_bytes=64 * 1024 * 1024
        ),
        cost_estimate=pl.CostEstimate(
            flops=2 * 2 * LINES * rows * planes * slab * width,
            bytes_accessed=6 * 1024 * 1024,
            transcendentals=0,
        ),
    )(
        owner_key,
        routes.transpose(0, 2, 1),
        mix_weights.transpose(0, 2, 1),
        counts,
        tokens.reshape(rows, model),
        up_partial[0, 0],
        down_partial[0, 0],
        up_master[0],
        down_master[0],
        up_first[0],
        down_first[0],
        up_second[0],
        down_second[0],
    )
    out_shapes = [((slab, width), f32), ((units, columns), f32), ((rows, columns), bf16)]
    up_update, down_update, decoded = pl.pallas_call(
        hand_out,
        out_shape=tuple(jax.ShapeDtypeStruct(*shape) for shape in out_shapes),
        in_specs=[hbm] * 4,
        out_specs=(hbm,) * 3,
        scratch_shapes=[pltpu.VMEM(r.shape, r.dtype) for r in results]
        + [pltpu.VMEM((rows, columns), bf16), pltpu.SemaphoreType.DMA((7,))],
        compiler_params=pltpu.CompilerParams(vmem_limit_bytes=64 * 1024 * 1024),
    )(*results)
    return (up_update[None], down_update[None], decoded.reshape(steps, rows_dev, columns))


def solution(mesh):
    return jax.shard_map(
        per_device,
        mesh=mesh,
        in_specs=(
            P(None, "expert", None),
            P(None, "expert", None),
            P(None, "expert", None),
            P("dp", "expert", None, None),
            P("dp", "expert", None, None),
            P("expert", None, "dp"),
            P("expert", None, "dp"),
            P("expert", None, "dp"),
            P("expert", None, "dp"),
            P("expert", None, "dp"),
            P("expert", None, "dp"),
            P("dp", None),
            P(),
        ),
        out_specs=(P("expert", None, "dp"), P("expert", None, "dp"), P(None, "expert", "dp")),
        check_vma=False,
    )
```
